256 devices in a mesh: fsdp: 32 (over x, y, core), tensor: 8 (over z).
Axes of the slice: x: 4, y: 4, z: 8, core: 2. Of those that a mesh axis runs over, the one named last changes fastest.
Arguments:
- weight_q: bfloat16 [16384, 16384], P('fsdp', 'tensor'), may hold values from -6 to 6
- momentum_q: bfloat16 [16384, 16384], P('fsdp', 'tensor'), may hold values from -6 to 6
- grad_q: bfloat16 [16384, 16384], P('fsdp', 'tensor'), may hold values from -12 to 12
- basis_q: float32 [16384, 128], P(('tensor', 'fsdp')), may hold values from -0.046875 to 0.046875
- weight_k: bfloat16 [16384, 1024], P('fsdp', 'tensor'), may hold values from -6 to 6
- momentum_k: bfloat16 [16384, 1024], P('fsdp', 'tensor'), may hold values from -6 to 6
- grad_k: bfloat16 [16384, 1024], P('fsdp', 'tensor'), may hold values from -12 to 12
- basis_k: float32 [1024, 128], P(('tensor', 'fsdp')), may hold values from -0.1875 to 0.1875
- weight_v: bfloat16 [16384, 1024], P('fsdp', 'tensor'), may hold values from -6 to 6
- momentum_v: bfloat16 [16384, 1024], P('fsdp', 'tensor'), may hold values from -6 to 6
- grad_v: bfloat16 [16384, 1024], P('fsdp', 'tensor'), may hold values from -12 to 12
- basis_v: float32 [1024, 128], P(('tensor', 'fsdp')), may hold values from -0.1875 to 0.1875
Outputs:
- new_weight_q: bfloat16 [16384, 16384], P('fsdp', 'tensor')
- new_momentum_q: bfloat16 [16384, 16384], P('fsdp', 'tensor')
- new_basis_q: float32 [16384, 128], P(('tensor', 'fsdp'))
- new_weight_k: bfloat16 [16384, 1024], P('fsdp', 'tensor')
- new_momentum_k: bfloat16 [16384, 1024], P('fsdp', 'tensor')
- new_basis_k: float32 [1024, 128], P(('tensor', 'fsdp'))
- new_weight_v: bfloat16 [16384, 1024], P('fsdp', 'tensor')
- new_momentum_v: bfloat16 [16384, 1024], P('fsdp', 'tensor')
- new_basis_v: float32 [1024, 128], P(('tensor', 'fsdp'))
The draws below stay inside these ranges and needn't reach their ends.
All inputs are finite; a program needn't handle non-finite values.
Results may differ from the reference program's by a relative error of at most 0.0017.
Values sent between devices are 32-bit elements; how exact they have to be, the bound alone decides.
No kernel may reach another device: no remote copies, remote signals or barrier semaphores. Data moves between devices by JAX's collectives and lax.ppermute only.
A program may use at most 64 MiB of HBM per device.

```python
import math
import jax
import jax.numpy as jnp
from jax import lax

D = 16384
RANK = 128
QW = 16384
KVW = 1024


def strengthened(values, own_key, source, target, shards_of, factor):
    owner, partner = [(jnp.arange(values.shape[axis_at]) // (values.shape[axis_at] // shards_of)).reshape([-1 if axis == axis_at else 1 for axis in range(values.ndim)]) for axis_at in (source, target)]
    chosen = jax.random.permutation(own_key, shards_of)[partner]
    strong = (owner == chosen) | (owner == (partner + shards_of // 2) % shards_of)
    return jnp.where(strong, factor * values, values)


def level_of(stream_key, shape, split, least, high):
    def one(axis_at, shards_of):
        steps = jax.random.uniform(jax.random.fold_in(jax.random.fold_in(stream_key, 6), axis_at), (shards_of,), jnp.float32, least / len(split), high / len(split))
        return jnp.repeat(jnp.exp(steps), shape[axis_at] // shards_of).reshape((-1,) + (1,) * (len(shape) - axis_at - 1))

    gain = one(*split[0])
    for cut in split[1:]:
        gain = gain * one(*cut)
    return gain


def scatter_about(own_key, dims, deviation, limit, shards=(), dtype=jnp.bfloat16):
    drawn = deviation * jax.random.normal(own_key, dims, jnp.float32)
    if shards:
        drawn = drawn * level_of(own_key, dims, shards, -0.22, 0.18)
    return jnp.clip(drawn, -limit, limit).astype(dtype)


def heavy_noise(key, shape, width, limit, cuts, heavy, dtype=jnp.bfloat16):
    entries = width * jax.random.normal(key, shape, jnp.float32)
    if cuts:
        entries = entries * level_of(key, shape, cuts, -0.22, 0.18)
    return jnp.clip(strengthened(entries, jax.random.fold_in(key, 3), *heavy), -limit, limit).astype(dtype)


def setup_inputs(seed: int = 0) -> dict:
    keys = jax.random.split(jax.random.key(seed), 13)
    return {
        "weight_q": scatter_about(keys[0], (D, QW), 1.0, 6.0, ((0, 32), (1, 8))),
        "momentum_q": scatter_about(keys[1], (D, QW), 1.0, 6.0, ((0, 32), (1, 8))),
        "grad_q": heavy_noise(keys[2], (D, QW), 1.0, 12.0, ((0, 32), (1, 8)), (0, 1, 32, 2.75)),
        "basis_q": scatter_about(keys[3], (QW, RANK), QW ** -0.5, 0.046875, ((0, 256),), jnp.float32),
        "weight_k": scatter_about(keys[4], (D, KVW), 1.0, 6.0, ((0, 32), (1, 8))),
        "momentum_k": scatter_about(keys[5], (D, KVW), 1.0, 6.0, ((0, 32), (1, 8))),
        "grad_k": heavy_noise(keys[6], (D, KVW), 1.0, 12.0, ((0, 32), (1, 8)), (0, 1, 32, 2.75)),
        "basis_k": scatter_about(keys[7], (KVW, RANK), KVW ** -0.5, 0.1875, ((0, 256),), jnp.float32),
        "weight_v": scatter_about(keys[8], (D, KVW), 1.0, 6.0, ((0, 32), (1, 8))),
        "momentum_v": scatter_about(keys[9], (D, KVW), 1.0, 6.0, ((0, 32), (1, 8))),
        "grad_v": heavy_noise(keys[10], (D, KVW), 1.0, 12.0, ((0, 32), (1, 8)), (0, 1, 32, 2.75)),
        "basis_v": scatter_about(keys[11], (KVW, RANK), KVW ** -0.5, 0.1875, ((0, 256),), jnp.float32),
    }


HIGH = lax.Precision.HIGHEST

def step_matrix(weight, momentum, grad, basis):
    blend = momentum.astype(jnp.float32) + grad.astype(jnp.float32)
    projected = jnp.dot(blend, basis, precision=HIGH)
    gram = jnp.dot(projected.T, projected, precision=HIGH)
    lower = jnp.linalg.cholesky(gram)
    ortho = jax.scipy.linalg.solve_triangular(lower, projected.T, lower=True).T
    right = jnp.dot(blend.T, ortho, precision=HIGH)
    inverse = lax.rsqrt(lax.optimization_barrier(jnp.sum(right * right, axis=0)) + 1e-06)
    new_basis = right * inverse
    new_momentum = (blend - 0.5 * jnp.dot(ortho, right.T, precision=HIGH)).astype(jnp.bfloat16)
    factor = 0.25 * math.sqrt(weight.shape[0] * weight.shape[1] / RANK)
    update = jnp.dot(ortho, new_basis.T, precision=HIGH)
    new_weight = (weight.astype(jnp.float32) - factor * update).astype(jnp.bfloat16)
    return (new_weight, new_momentum, new_basis)

def reference(weight_q, momentum_q, grad_q, basis_q, weight_k, momentum_k, grad_k, basis_k, weight_v, momentum_v, grad_v, basis_v):
    wq, mq, bq = step_matrix(weight_q, momentum_q, grad_q, basis_q)
    wk, mk, bk = step_matrix(weight_k, momentum_k, grad_k, basis_k)
    wv, mv, bv = step_matrix(weight_v, momentum_v, grad_v, basis_v)
    return (wq, mq, bq, wk, mk, bk, wv, mv, bv)
```

```python
import math

import jax
import jax.numpy as jnp
from jax import lax
from jax.sharding import PartitionSpec as P

RANK = 128
HIGH = lax.Precision.HIGHEST
PLANE = [[2 * i + c for i in range(16)] for c in range(2)]
SIBLING = [(i, i ^ 1) for i in range(32)]


def swap_core(x):
    return lax.ppermute(x, "fsdp", SIBLING)


def plane_exchange(x):
    return lax.all_to_all(x, "fsdp", 0, 0, tiled=True, axis_index_groups=PLANE)


def tensor_exchange(x):
    return lax.all_to_all(x, "tensor", 0, 0, tiled=True)


def gather_fsdp(x, core):
    mine = plane_exchange(jnp.broadcast_to(x[None], (16,) + x.shape))
    other = swap_core(mine)
    low = jnp.where(core == 0, mine, other)
    high = jnp.where(core == 0, other, mine)
    return jnp.stack([low, high], axis=1)


def scatter_fsdp(x, core):
    keep = jnp.where(core == 0, x[:, 0], x[:, 1])
    send = jnp.where(core == 0, x[:, 1], x[:, 0])
    paired = keep + swap_core(send)
    return jnp.sum(plane_exchange(paired), axis=0)


def body(
    weight_q,
    momentum_q,
    grad_q,
    basis_q,
    weight_k,
    momentum_k,
    grad_k,
    basis_k,
    weight_v,
    momentum_v,
    grad_v,
    basis_v,
):
    weights = (weight_q, weight_k, weight_v)
    moments = (momentum_q, momentum_k, momentum_v)
    grads = (grad_q, grad_k, grad_v)
    fsdp = lax.axis_index("fsdp")
    core = lax.rem(fsdp, 2)

    packed = jnp.concatenate([basis_q, basis_k, basis_v], axis=0)
    bases = gather_fsdp(packed, core).reshape(32, 72, RANK)
    bases = (
        bases[:, :64].reshape(2048, RANK),
        bases[:, 64:68].reshape(128, RANK),
        bases[:, 68:].reshape(128, RANK),
    )
    blends = [m.astype(jnp.float32) + g.astype(jnp.float32) for m, g in zip(moments, grads)]
    partial_rows = jnp.concatenate(
        [jnp.dot(b, q, precision=HIGH).reshape(8, 64, RANK) for b, q in zip(blends, bases)], axis=1
    )
    own_rows = jnp.sum(tensor_exchange(partial_rows), axis=0)
    rows = lax.all_gather(own_rows, "tensor", axis=0)
    projected = [rows[:, 64 * i : 64 * i + 64].reshape(512, RANK) for i in range(3)]

    rights = [jnp.dot(b.T, p, precision=HIGH) for b, p in zip(blends, projected)]
    grams = [jnp.dot(p.T, p, precision=HIGH) for p in projected]
    pad = jnp.zeros((128, RANK), jnp.float32)
    full = jnp.concatenate(rights + grams + [pad], axis=0)
    share = scatter_fsdp(full.reshape(16, 2, 88, RANK), core)
    full = gather_fsdp(share, core).reshape(2816, RANK)
    rights = (full[:2048], full[2048:2176], full[2176:2304])
    grams = full[2304:2688].reshape(3, RANK, RANK)

    lowers = jnp.linalg.cholesky(grams)
    eye = jnp.broadcast_to(jnp.eye(RANK, dtype=jnp.float32), grams.shape)
    inverse_lowers = jax.scipy.linalg.solve_triangular(lowers, eye, lower=True)
    orthos = [jnp.dot(p, li.T, precision=HIGH) for p, li in zip(projected, inverse_lowers)]
    rights = [jnp.dot(r, li.T, precision=HIGH) for r, li in zip(rights, inverse_lowers)]
    squares = jnp.stack([jnp.sum(r * r, axis=0) for r in rights])
    squares = jnp.sum(tensor_exchange(jnp.broadcast_to(squares[None], (8, 3, RANK))), axis=0)
    inverses = lax.rsqrt(squares + 1e-06)
    results = []
    for i in range(3):
        w, b, o, r = weights[i], blends[i], orthos[i], rights[i]
        new_momentum = (b - 0.5 * jnp.dot(o, r.T, precision=HIGH)).astype(jnp.bfloat16)
        rows_all = w.shape[0] * lax.axis_size("fsdp")
        cols_all = w.shape[1] * lax.axis_size("tensor")
        factor = 0.25 * math.sqrt(rows_all * cols_all / RANK)
        basis = r * inverses[i]
        update = jnp.dot(o, basis.T, precision=HIGH)
        new_weight = (w.astype(jnp.float32) - factor * update).astype(jnp.bfloat16)
        own = basis.shape[0] // 32
        results.extend([new_weight, new_momentum, lax.dynamic_slice_in_dim(basis, fsdp * own, own)])
    return tuple(results)


def solution(mesh):
    placed = (
        P("fsdp", "tensor"),
        P("fsdp", "tensor"),
        P("fsdp", "tensor"),
        P(("tensor", "fsdp"), None),
    ) * 3
    return jax.shard_map(
        body,
        mesh=mesh,
        in_specs=placed,
        out_specs=(
            P("fsdp", "tensor"),
            P("fsdp", "tensor"),
            P(("tensor", "fsdp"), None),
        )
        * 3,
        check_vma=False,
    )
```

```python
import functools
import math

import jax
import jax.numpy as jnp
from jax import lax
from jax.experimental import pallas as pl
from jax.experimental.pallas import tpu as pltpu
from jax.sharding import PartitionSpec as P

RANK = 128
HIGHEST = lax.Precision.HIGHEST
F32 = jnp.float32
BF16 = jnp.bfloat16
PLANE = [[2 * i + c for i in range(16)] for c in range(2)]
SIBLING = [(i, i ^ 1) for i in range(32)]
STEPS = 4
BLOCKS = 22
HALF = BLOCKS // 2


def swap_core(x):
    return lax.ppermute(x, "fsdp", SIBLING)


def plane_exchange(x):
    return lax.all_to_all(x, "fsdp", 0, 0, tiled=True, axis_index_groups=PLANE)


def plane_gather(x):
    return plane_exchange(jnp.broadcast_to(x[None], (16,) + x.shape))


def tensor_exchange(x):
    return lax.all_to_all(x, "tensor", 0, 0, tiled=True)


def tensor_shift(x, distance):
    return lax.ppermute(x, "tensor", [(i, (i + distance) % 8) for i in range(8)])


def dot(a, b, contract=(1, 0)):
    dims = (((contract[0],), (contract[1],)), ((), ()))
    return lax.dot_general(a, b, dims, preferred_element_type=F32)


def split(x):
    high = x.astype(BF16)
    return high, (x - high.astype(F32)).astype(BF16)


def blend_of(moment_ref, grad_ref):
    return moment_ref[...].astype(F32) + grad_ref[...].astype(F32)


def full_spec(shape):
    return pl.BlockSpec(shape, lambda i: (0,) * len(shape))


def column_spec(rows):
    return pl.BlockSpec((rows, 2048 // STEPS), lambda i: (0, i))


SMEM = pl.BlockSpec(memory_space=pltpu.SMEM)


def rows_kernel(
    place, mq, gq, mine, other, mk, gk, mv, gv, out, rows, small
):
    step = pl.program_id(0)
    chips = 16 // STEPS
    first = place[2] == 0
    a, b = mine[...], other[...]
    low, high = jnp.where(first, a, b), jnp.where(first, b, a)

    def times(blend, basis):
        bh, bl = split(blend)
        qh, ql = split(basis)
        both = dot(bh, jnp.concatenate([qh, ql], axis=1))
        return both[:, :RANK] + both[:, RANK:] + dot(bl, qh)

    pieces = []
    for i in range(chips):
        pieces += [low[i, :64], high[i, :64]]
        at = pl.multiple_of((step * chips + i) * 8, 8)
        small[0, pl.ds(at, 8)] = jnp.concatenate([low[i, 64:68], high[i, 64:68]], axis=0)
        small[1, pl.ds(at, 8)] = jnp.concatenate([low[i, 68:72], high[i, 68:72]], axis=0)
    part = times(blend_of(mq, gq), jnp.concatenate(pieces, axis=0))

    @pl.when(step == 0)
    def _():
        rows[0] = part

    @pl.when(step > 0)
    def _():
        rows[0] += part

    @pl.when(step == STEPS - 1)
    def _():
        rows[1] = times(blend_of(mk, gk), small[0])
        rows[2] = times(blend_of(mv, gv), small[1])
        for d in range(8):
            for m in range(3):
                out[d, 64 * m : 64 * m + 64] = rows[m, 64 * d : 64 * d + 64]


def partial_rows(place, moments, grads, mine, other):
    tall = full_spec((512, RANK))
    gathered = pl.BlockSpec((16 // STEPS, 72, RANK), lambda i: (i, 0, 0))
    return pl.pallas_call(
        rows_kernel,
        grid=(STEPS,),
        in_specs=[SMEM, column_spec(512), column_spec(512), gathered, gathered] + [tall] * 4,
        out_specs=full_spec((8, 192, RANK)),
        out_shape=jax.ShapeDtypeStruct((8, 192, RANK), F32),
        scratch_shapes=[pltpu.VMEM((3, 512, RANK), F32), pltpu.VMEM((2, RANK, RANK), F32)],
        cost_estimate=pl.CostEstimate(
            flops=6 * 512 * 2304 * RANK, bytes_accessed=7_000_000, transcendentals=0
        ),
        name="partial_rows",
    )(place, moments[0], grads[0], mine, other, moments[1], grads[1], moments[2], grads[2])


def right_kernel(
    place, mq, gq, mk, gk, mv, gv, r0, r1, r2, r3, r4, r5, r6, r7, keep, send, projected, lhs
):
    step = pl.program_id(0)
    core = place[2]

    def put(half, at, value):
        @pl.when(half == core)
        def _():
            keep[at] = value

        @pl.when(half != core)
        def _():
            send[at] = value

    def times(m, blend):
        bh, bl = split(blend)
        both = dot(lhs[m], bh)
        return both[:RANK] + both[RANK:] + dot(lhs[m, :RANK], bl)

    @pl.when(step == 0)
    def _():
        for d, rows in enumerate((r0, r1, r2, r3, r4, r5, r6, r7)):
            at = pl.multiple_of(lax.rem(place[0] + (8 - d), 8) * 64, 64)
            for m in range(3):
                projected[m, pl.ds(at, 64)] = rows[64 * m : 64 * m + 64]
        for m in range(3):
            p = projected[m]
            turned = p.T
            high, low = split(turned)
            lhs[m, :RANK] = high
            lhs[m, RANK:] = low
            gram = jnp.dot(turned, p, precision=HIGHEST, preferred_element_type=F32)
            put(1, 18 + m - HALF, gram)
        put(1, 16 - HALF, times(1, blend_of(mk, gk)))
        put(1, 17 - HALF, times(2, blend_of(mv, gv)))
        put(1, 21 - HALF, jnp.zeros((RANK, RANK), F32))

    right = times(0, blend_of(mq, gq))
    for i in range(16 // STEPS):
        at = step * (16 // STEPS) + i
        put(at // HALF, lax.rem(at, HALF), right[:, RANK * i : RANK * i + RANK])


def right_parts(place, moments, grads, rows):
    tall = full_spec((512, RANK))
    half = (HALF, RANK, RANK)
    return pl.pallas_call(
        right_kernel,
        grid=(STEPS,),
        in_specs=[SMEM, column_spec(512), column_spec(512)] + [tall] * 4 + [full_spec((192, RANK))] * 8,
        out_specs=[full_spec(half), full_spec(half), full_spec((3, 512, RANK))],
        out_shape=[
            jax.ShapeDtypeStruct(half, F32),
            jax.ShapeDtypeStruct(half, F32),
            jax.ShapeDtypeStruct((3, 512, RANK), F32),
        ],
        scratch_shapes=[pltpu.VMEM((3, 2 * RANK, 512), BF16)],
        cost_estimate=pl.CostEstimate(
            flops=6 * 512 * 2304 * RANK, bytes_accessed=8_000_000, transcendentals=0
        ),
        name="right_parts",
    )(place, moments[0], grads[0], moments[1], grads[1], moments[2], grads[2], *rows)


def eliminate(work):
    sub = lax.broadcasted_iota(jnp.int32, (8, RANK), 0)
    for p in range(16):
        lo = 8 * p
        for m in range(3):
            panel = work[m, lo : lo + 8, :]
            if p > 0:
                coef = work[m, :lo, :RANK][:, lo : lo + 8]
                panel = panel - lax.dot_general(
                    coef,
                    work[m, :lo, :],
                    (((0,), (0,)), ((), ())),
                    precision=HIGHEST,
                    preferred_element_type=F32,
                )
            cols = [jnp.broadcast_to(panel[:, lo + k : lo + k + 1], (8, RANK)) for k in range(8)]
            left, right = panel[:, :RANK], panel[:, RANK:]
            for j in range(8):
                inv = lax.rsqrt(jnp.broadcast_to(cols[j][j : j + 1, :], (8, RANK)))
                row_left = jnp.broadcast_to(left[j : j + 1, :], (8, RANK)) * inv
                row_right = jnp.broadcast_to(right[j : j + 1, :], (8, RANK)) * inv
                below = jnp.where(sub > j, cols[j] * inv, 0.0)
                for k in range(j + 1, 8):
                    cols[k] = cols[k] - below * (jnp.broadcast_to(cols[k][j : j + 1, :], (8, RANK)) * inv)
                left = jnp.where(sub == j, row_left, left - below * row_left)
                right = jnp.where(sub == j, row_right, right - below * row_right)
            work[m, lo : lo + 8, :RANK] = left
            work[m, lo : lo + 8, RANK:] = right


def factor_kernel(
    place, mine, other, projected, ortho, right_high, right_low, squares, sq, sk, sv, work, turned
):
    core = place[2]
    fsdp = place[1]

    def block(j):
        return jnp.where(core == j // HALF, mine[j % HALF], other[j % HALF])

    row = lax.broadcasted_iota(jnp.int32, (RANK, RANK), 0)
    col = lax.broadcasted_iota(jnp.int32, (RANK, RANK), 1)
    for m in range(3):
        work[m, :, :RANK] = block(18 + m)
        work[m, :, RANK:] = jnp.where(row == col, 1.0, 0.0).astype(F32)
    eliminate(work)
    for m, blocks in enumerate((range(16), (16,), (17,))):
        inverse = work[m, :, RANK:]
        ih, il = split(inverse)
        ph, plow = split(projected[m])
        ortho[m] = dot(ph, ih, (1, 1)) + dot(ph, il, (1, 1)) + dot(plow, ih, (1, 1))
        stacked = jnp.concatenate([ih, il], axis=0)
        total = jnp.zeros((RANK, RANK), F32)
        for j in blocks:
            zh, zl = split(block(j))
            both = dot(stacked, zh)
            right = both[:RANK] + both[RANK:] + dot(ih, zl)
            total += right * right
            high, low = split(right)
            right_high[:, RANK * j : RANK * j + RANK] = high
            right_low[:, RANK * j : RANK * j + RANK] = low
            if m == 0:
                @pl.when(lax.div(fsdp, 2) == j)
                def _():
                    turned[0] = right.T
            else:
                turned[m] = right.T
        sums = jnp.sum(total.T, axis=0, keepdims=True)
        for d in range(8):
            squares[d, m : m + 1, :] = sums
    for d in range(8):
        squares[d, 3:, :] = jnp.zeros((5, RANK), F32)
    odd = lax.rem(fsdp, 2)
    sq[...] = turned[0, pl.ds(pl.multiple_of(odd * 64, 64), 64)]
    for m, out in ((1, sk), (2, sv)):
        tile = turned[m, pl.ds(pl.multiple_of(lax.div(fsdp, 2) * 8, 8), 8)]
        out[...] = jnp.where(odd == 0, tile[:4], tile[4:])


def factor_and_rotate(place, mine, other, projected):
    vmem = pl.BlockSpec(memory_space=pltpu.VMEM)
    return pl.pallas_call(
        factor_kernel,
        in_specs=[SMEM, vmem, vmem, vmem],
        out_specs=[vmem] * 7,
        out_shape=[
            jax.ShapeDtypeStruct((3, 512, RANK), F32),
            jax.ShapeDtypeStruct((RANK, 2304), BF16),
            jax.ShapeDtypeStruct((RANK, 2304), BF16),
            jax.ShapeDtypeStruct((8, 8, RANK), F32),
            jax.ShapeDtypeStruct((64, RANK), F32),
            jax.ShapeDtypeStruct((4, RANK), F32),
            jax.ShapeDtypeStruct((4, RANK), F32),
        ],
        scratch_shapes=[pltpu.VMEM((3, RANK, 2 * RANK), F32), pltpu.VMEM((3, RANK, RANK), F32)],
        name="factor_and_rotate",
    )(place, mine, other, projected)


def store_split(lhs, m, value):
    high, low = split(value)
    lhs[m, :, :RANK] = high
    lhs[m, :, RANK:] = low


def minus_product(base, lhs, m, high, low):
    product = dot(lhs[m], jnp.concatenate([high, high], axis=0)) + dot(lhs[m, :, :RANK], low)
    return (base - product).astype(BF16)


def momentum_kernel(
    mq, gq, mk, gk, mv, gv, ortho, hq, lq, hs, ls, out_q, out_k, out_v, lhs
):
    @pl.when(pl.program_id(0) == 0)
    def _():
        for m in range(3):
            store_split(lhs, m, 0.5 * ortho[m])
        out_k[...] = minus_product(blend_of(mk, gk), lhs, 1, hs[:, :RANK], ls[:, :RANK])
        out_v[...] = minus_product(blend_of(mv, gv), lhs, 2, hs[:, RANK:], ls[:, RANK:])

    out_q[...] = minus_product(blend_of(mq, gq), lhs, 0, hq[...], lq[...])


def weight_kernel(
    factors, wq, wk, wv, ortho, hq, lq, hs, ls, squares, sq, sk, sv,
    out_q, out_k, out_v, bq, bk, bv, lhs,
):
    @pl.when(pl.program_id(0) == 0)
    def _():
        inverse = lax.rsqrt(jnp.sum(squares[...], axis=0) + 1e-06)
        for m in range(3):
            store_split(lhs, m, ortho[m] * (factors[m] * inverse[m : m + 1]))
        for m, share, out in ((0, sq, bq), (1, sk, bk), (2, sv, bv)):
            out[...] = share[...] * inverse[m : m + 1]
        out_k[...] = minus_product(wk[...].astype(F32), lhs, 1, hs[:, :RANK], ls[:, :RANK])
        out_v[...] = minus_product(wv[...].astype(F32), lhs, 2, hs[:, RANK:], ls[:, RANK:])

    out_q[...] = minus_product(wq[...].astype(F32), lhs, 0, hq[...], lq[...])


TALL = full_spec((512, RANK))
ORTHO = full_spec((3, 512, RANK))
SMALL_RIGHT = pl.BlockSpec((RANK, 2 * RANK), lambda i: (0, 8))
WIDE_OUT = [
    jax.ShapeDtypeStruct((512, 2048), BF16),
    jax.ShapeDtypeStruct((512, RANK), BF16),
    jax.ShapeDtypeStruct((512, RANK), BF16),
]
COST = pl.CostEstimate(flops=6 * 512 * 2304 * RANK, bytes_accessed=9_000_000, transcendentals=0)


def new_momenta(moments, grads, ortho, high, low):
    wide = column_spec(512)
    return pl.pallas_call(
        momentum_kernel,
        grid=(STEPS,),
        in_specs=[wide, wide] + [TALL] * 4 + [ORTHO, column_spec(RANK), column_spec(RANK), SMALL_RIGHT, SMALL_RIGHT],
        out_specs=[wide, TALL, TALL],
        out_shape=WIDE_OUT,
        scratch_shapes=[pltpu.VMEM((3, 512, 2 * RANK), BF16)],
        cost_estimate=COST,
        name="new_momenta",
    )(moments[0], grads[0], moments[1], grads[1], moments[2], grads[2], ortho, high, low, high, low)


def new_weights(factors, weights, ortho, high, low, squares, shares):
    wide = column_spec(512)
    share_specs = [full_spec((64, RANK)), full_spec((4, RANK)), full_spec((4, RANK))]
    return pl.pallas_call(
        functools.partial(weight_kernel, factors),
        grid=(STEPS,),
        in_specs=[wide, TALL, TALL, ORTHO, column_spec(RANK), column_spec(RANK), SMALL_RIGHT, SMALL_RIGHT]
        + [full_spec((8, 8, RANK))]
        + share_specs,
        out_specs=[wide, TALL, TALL] + share_specs,
        out_shape=WIDE_OUT + [jax.ShapeDtypeStruct(s.block_shape, F32) for s in share_specs],
        scratch_shapes=[pltpu.VMEM((3, 512, 2 * RANK), BF16)],
        cost_estimate=COST,
        name="new_weights",
    )(*weights, ortho, high, low, high, low, squares, *shares)


def body(
    weight_q,
    momentum_q,
    grad_q,
    basis_q,
    weight_k,
    momentum_k,
    grad_k,
    basis_k,
    weight_v,
    momentum_v,
    grad_v,
    basis_v,
):
    weights = (weight_q, weight_k, weight_v)
    moments = (momentum_q, momentum_k, momentum_v)
    grads = (grad_q, grad_k, grad_v)
    fsdp = lax.axis_index("fsdp")
    place = jnp.stack([lax.axis_index("tensor"), fsdp, lax.rem(fsdp, 2)]).astype(jnp.int32)
    factors = [
        0.25 * math.sqrt(w.shape[0] * lax.axis_size("fsdp") * w.shape[1] * lax.axis_size("tensor") / RANK)
        for w in weights
    ]

    mine = plane_gather(jnp.concatenate([basis_q, basis_k, basis_v], axis=0))
    chunks = partial_rows(place, moments, grads, mine, swap_core(mine))
    own = jnp.sum(tensor_exchange(chunks), axis=0)
    rows = [own] + [tensor_shift(own, d) for d in range(1, 8)]
    keep, send, projected = right_parts(place, moments, grads, rows)

    paired = (keep + swap_core(send)).reshape(16, 88, RANK)
    mine = plane_gather(jnp.sum(plane_exchange(paired), axis=0)).reshape(HALF, RANK, RANK)
    ortho, high, low, squares, *shares = factor_and_rotate(place, mine, swap_core(mine), projected)
    squares = tensor_exchange(squares)
    momenta = new_momenta(moments, grads, ortho, high, low)
    new_w = new_weights(factors, weights, ortho, high, low, squares, shares)
    return tuple(x for i in range(3) for x in (new_w[i], momenta[i], new_w[3 + i]))


def solution(mesh):
    placed = (
        P("fsdp", "tensor"),
        P("fsdp", "tensor"),
        P("fsdp", "tensor"),
        P(("tensor", "fsdp"), None),
    ) * 3
    return jax.shard_map(
        body,
        mesh=mesh,
        in_specs=placed,
        out_specs=(
            P("fsdp", "tensor"),
            P("fsdp", "tensor"),
            P(("tensor", "fsdp"), None),
        )
        * 3,
        check_vma=False,
    )
```

```python
import functools
import math

import jax
import jax.numpy as jnp
from jax import lax
from jax.experimental import pallas as pl
from jax.experimental.pallas import tpu as pltpu
from jax.sharding import PartitionSpec as P

RANK = 128
HIGHEST = lax.Precision.HIGHEST
F32 = jnp.float32
BF16 = jnp.bfloat16
PLANE = [[2 * i + c for i in range(16)] for c in range(2)]
SIBLING = [(i, i ^ 1) for i in range(32)]
STEPS = 4
BLOCKS = 22
HALF = BLOCKS // 2
VMEM_LIMIT = 24 * 1024 * 1024


def swap_core(x):
    return lax.ppermute(x, "fsdp", SIBLING)


def plane_exchange(x):
    return lax.all_to_all(x, "fsdp", 0, 0, tiled=True, axis_index_groups=PLANE)


def plane_gather(x):
    return plane_exchange(jnp.broadcast_to(x[None], (16,) + x.shape))


def tensor_exchange(x):
    return lax.all_to_all(x, "tensor", 0, 0, tiled=True)


def tensor_shift(x, distance):
    return lax.ppermute(x, "tensor", [(i, (i + distance) % 8) for i in range(8)])


def dot(a, b, contract=(1, 0)):
    dims = (((contract[0],), (contract[1],)), ((), ()))
    return lax.dot_general(a, b, dims, preferred_element_type=F32)


def split(x):
    high = x.astype(BF16)
    return high, (x - high.astype(F32)).astype(BF16)


def blend_of(moment_ref, grad_ref):
    return moment_ref[...].astype(F32) + grad_ref[...].astype(F32)


def full_spec(shape):
    return pl.BlockSpec(shape, lambda i: (0,) * len(shape))


def column_spec(rows):
    return pl.BlockSpec((rows, 2048 // STEPS), lambda i: (0, i))


VMEM = pl.BlockSpec(memory_space=pltpu.VMEM)


def blend_kernel(mq, gq, mk, gk, mv, gv, high, low):
    for at, moment, grad in ((0, mq, gq), (2048, mk, gk), (2048 + RANK, mv, gv)):
        h, l = split(moment[...].astype(F32) + grad[...].astype(F32))
        span = slice(at, at + h.shape[1])
        high[:, span] = h
        low[:, span] = l


def blend_terms(moments, grads):
    def rows(width):
        return pl.BlockSpec((128, width), lambda i: (i, 0))

    return pl.pallas_call(
        blend_kernel,
        grid=(4,),
        in_specs=[rows(2048)] * 2 + [rows(RANK)] * 4,
        out_specs=[rows(2304)] * 2,
        out_shape=[jax.ShapeDtypeStruct((512, 2304), BF16)] * 2,
        compiler_params=pltpu.CompilerParams(vmem_limit_bytes=VMEM_LIMIT),
        cost_estimate=pl.CostEstimate(
            flops=4 * 512 * 2304, bytes_accessed=9_400_000, transcendentals=0
        ),
        name="blend_terms",
    )(*(x for group in zip(moments, grads) for x in group))


def small_kernel(kernel, shape, name, *operands):
    return pl.pallas_call(
        kernel,
        in_specs=[VMEM] * len(operands),
        out_specs=VMEM,
        out_shape=jax.ShapeDtypeStruct(shape, F32),
        compiler_params=pltpu.CompilerParams(vmem_limit_bytes=VMEM_LIMIT),
        name=name,
    )(*operands)


def total_kernel(parts, out):
    out[...] = jnp.sum(parts[...], axis=0)


def repeat_total_kernel(parts, out):
    total = jnp.sum(parts[...], axis=0)
    for i in range(16):
        out[i] = total


def pair_kernel(a, b, out):
    out[...] = a[...] + b[...]


def rows_kernel(high, low, mine, other, out, basis, small):
    first = lax.rem(lax.axis_index("fsdp"), 2) == 0
    for i in range(16):
        a, b = mine[i], other[i]
        pair = (jnp.where(first, a, b), jnp.where(first, b, a))
        for c in range(2):
            at = 128 * i + 64 * c
            qh, ql = split(pair[c][:64])
            basis[at : at + 64, :RANK] = qh
            basis[at : at + 64, RANK:] = ql
        for n in range(2):
            piece = [x[64 + 4 * n : 68 + 4 * n] for x in pair]
            small[n, 8 * i : 8 * i + 8] = jnp.concatenate(piece, axis=0)
    for n in range(2):
        qh, ql = split(small[n])
        basis[2048 + RANK * n : 2048 + RANK * n + RANK, :RANK] = qh
        basis[2048 + RANK * n : 2048 + RANK * n + RANK, RANK:] = ql
    for m, (lo, hi) in enumerate(((0, 2048), (2048, 2176), (2176, 2304))):
        for half in range(2):
            at = slice(256 * half, 256 * half + 256)
            both = dot(high[at, lo:hi], basis[lo:hi])
            rows = both[:, :RANK] + both[:, RANK:] + dot(low[at, lo:hi], basis[lo:hi, :RANK])
            for d in range(4):
                out[4 * half + d, 64 * m : 64 * m + 64] = rows[64 * d : 64 * d + 64]


def partial_rows(high, low, mine, other):
    return pl.pallas_call(
        rows_kernel,
        in_specs=[VMEM] * 4,
        out_specs=VMEM,
        out_shape=jax.ShapeDtypeStruct((8, 192, RANK), F32),
        scratch_shapes=[pltpu.VMEM((2304, 2 * RANK), BF16), pltpu.VMEM((2, RANK, RANK), F32)],
        compiler_params=pltpu.CompilerParams(vmem_limit_bytes=VMEM_LIMIT),
        cost_estimate=pl.CostEstimate(
            flops=6 * 512 * 2304 * RANK, bytes_accessed=7_000_000, transcendentals=0
        ),
        name="partial_rows",
    )(high, low, mine, other)


def right_kernel(
    high, low, r0, r1, r2, r3, r4, r5, r6, r7, keep, send, projected, lhs
):
    core = lax.rem(lax.axis_index("fsdp"), 2)
    tensor = lax.axis_index("tensor")

    def put(at, value):
        @pl.when(core == at // HALF)
        def _():
            keep[at % HALF] = value

        @pl.when(core != at // HALF)
        def _():
            send[at % HALF] = value

    def times(m, lo, hi):
        both = dot(lhs[m], high[:, lo:hi])
        return both[:RANK] + both[RANK:] + dot(lhs[m, :RANK], low[:, lo:hi])

    for d, rows in enumerate((r0, r1, r2, r3, r4, r5, r6, r7)):
        at = pl.multiple_of(lax.rem(tensor + (8 - d), 8) * 64, 64)
        for m in range(3):
            projected[m, pl.ds(at, 64)] = rows[64 * m : 64 * m + 64]
    for m in range(3):
        p = projected[m]
        turned = p.T
        h, l = split(turned)
        lhs[m, :RANK] = h
        lhs[m, RANK:] = l
        put(18 + m, jnp.dot(turned, p, precision=HIGHEST, preferred_element_type=F32))
    for lo in range(0, 2048, 512):
        right = times(0, lo, lo + 512)
        for i in range(4):
            put(lo // RANK + i, right[:, RANK * i : RANK * i + RANK])
    put(16, times(1, 2048, 2176))
    put(17, times(2, 2176, 2304))
    put(21, jnp.zeros((RANK, RANK), F32))


def right_parts(high, low, rows):
    half = (HALF, RANK, RANK)
    return pl.pallas_call(
        right_kernel,
        in_specs=[VMEM] * 10,
        out_specs=[VMEM] * 3,
        out_shape=[
            jax.ShapeDtypeStruct(half, F32),
            jax.ShapeDtypeStruct(half, F32),
            jax.ShapeDtypeStruct((3, 512, RANK), F32),
        ],
        scratch_shapes=[pltpu.VMEM((3, 2 * RANK, 512), BF16)],
        compiler_params=pltpu.CompilerParams(vmem_limit_bytes=VMEM_LIMIT),
        cost_estimate=pl.CostEstimate(
            flops=6 * 512 * 2304 * RANK, bytes_accessed=8_000_000, transcendentals=0
        ),
        name="right_parts",
    )(high, low, *rows)


def eliminate(work):
    sub = lax.broadcasted_iota(jnp.int32, (8, RANK), 0)
    for p in range(16):
        lo = 8 * p
        for m in range(3):
            panel = work[m, lo : lo + 8, :]
            if p > 0:
                coef = work[m, :lo, :RANK][:, lo : lo + 8]
                panel = panel - lax.dot_general(
                    coef,
                    work[m, :lo, :],
                    (((0,), (0,)), ((), ())),
                    precision=HIGHEST,
                    preferred_element_type=F32,
                )
            cols = [jnp.broadcast_to(panel[:, lo + k : lo + k + 1], (8, RANK)) for k in range(8)]
            left, right = panel[:, :RANK], panel[:, RANK:]
            for j in range(8):
                inv = lax.rsqrt(jnp.broadcast_to(cols[j][j : j + 1, :], (8, RANK)))
                row_left = jnp.broadcast_to(left[j : j + 1, :], (8, RANK)) * inv
                row_right = jnp.broadcast_to(right[j : j + 1, :], (8, RANK)) * inv
                below = jnp.where(sub > j, cols[j] * inv, 0.0)
                for k in range(j + 1, 8):
                    cols[k] = cols[k] - below * (jnp.broadcast_to(cols[k][j : j + 1, :], (8, RANK)) * inv)
                left = jnp.where(sub == j, row_left, left - below * row_left)
                right = jnp.where(sub == j, row_right, right - below * row_right)
            work[m, lo : lo + 8, :RANK] = left
            work[m, lo : lo + 8, RANK:] = right


def factor_kernel(
    mine, other, projected, ortho, right_high, right_low, squares, sq, sk, sv, work, turned
):
    fsdp = lax.axis_index("fsdp")
    core = lax.rem(fsdp, 2)

    def block(j):
        return jnp.where(core == j // HALF, mine[j % HALF], other[j % HALF])

    row = lax.broadcasted_iota(jnp.int32, (RANK, RANK), 0)
    col = lax.broadcasted_iota(jnp.int32, (RANK, RANK), 1)
    for m in range(3):
        work[m, :, :RANK] = block(18 + m)
        work[m, :, RANK:] = jnp.where(row == col, 1.0, 0.0).astype(F32)
    eliminate(work)
    for m, blocks in enumerate((range(16), (16,), (17,))):
        inverse = work[m, :, RANK:]
        ih, il = split(inverse)
        ph, plow = split(projected[m])
        ortho[m] = dot(ph, ih, (1, 1)) + dot(ph, il, (1, 1)) + dot(plow, ih, (1, 1))
        stacked = jnp.concatenate([ih, il], axis=0)
        total = jnp.zeros((RANK, RANK), F32)
        for j in blocks:
            zh, zl = split(block(j))
            both = dot(stacked, zh)
            right = both[:RANK] + both[RANK:] + dot(ih, zl)
            total += right * right
            high, low = split(right)
            right_high[:, RANK * j : RANK * j + RANK] = high
            right_low[:, RANK * j : RANK * j + RANK] = low
            if m == 0:
                @pl.when(lax.div(fsdp, 2) == j)
                def _():
                    turned[0] = right.T
            else:
                turned[m] = right.T
        sums = jnp.sum(total.T, axis=0, keepdims=True)
        for d in range(8):
            squares[d, m : m + 1, :] = sums
    for d in range(8):
        squares[d, 3:, :] = jnp.zeros((5, RANK), F32)
    odd = lax.rem(fsdp, 2)
    sq[...] = turned[0, pl.ds(pl.multiple_of(odd * 64, 64), 64)]
    for m, out in ((1, sk), (2, sv)):
        tile = turned[m, pl.ds(pl.multiple_of(lax.div(fsdp, 2) * 8, 8), 8)]
        out[...] = jnp.where(odd == 0, tile[:4], tile[4:])


def factor_and_rotate(mine, other, projected):
    return pl.pallas_call(
        factor_kernel,
        in_specs=[VMEM, VMEM, VMEM],
        out_specs=[VMEM] * 7,
        out_shape=[
            jax.ShapeDtypeStruct((3, 512, RANK), F32),
            jax.ShapeDtypeStruct((RANK, 2304), BF16),
            jax.ShapeDtypeStruct((RANK, 2304), BF16),
            jax.ShapeDtypeStruct((8, 8, RANK), F32),
            jax.ShapeDtypeStruct((64, RANK), F32),
            jax.ShapeDtypeStruct((4, RANK), F32),
            jax.ShapeDtypeStruct((4, RANK), F32),
        ],
        scratch_shapes=[pltpu.VMEM((3, RANK, 2 * RANK), F32), pltpu.VMEM((3, RANK, RANK), F32)],
        compiler_params=pltpu.CompilerParams(vmem_limit_bytes=VMEM_LIMIT),
        name="factor_and_rotate",
    )(mine, other, projected)


def store_split(lhs, m, value):
    high, low = split(value)
    lhs[m, :, :RANK] = high
    lhs[m, :, RANK:] = low


def minus_product(base, lhs, m, high, low):
    product = dot(lhs[m], jnp.concatenate([high, high], axis=0)) + dot(lhs[m, :, :RANK], low)
    return (base - product).astype(BF16)


def update_kernel(
    factors, high, low, wq, wk, wv, ortho, rh, rl, squares, sq, sk, sv,
    mq, mk, mv, out_q, out_k, out_v, bq, bk, bv, half, scaled,
):
    step = pl.program_id(0)

    def new(m, span, weight, moment_out, weight_out):
        base = high[:, span].astype(F32) + low[:, span].astype(F32)
        moment_out[...] = minus_product(base, half, m, rh[:, span], rl[:, span])
        weight_out[...] = minus_product(weight.astype(F32), scaled, m, rh[:, span], rl[:, span])

    @pl.when(step == 0)
    def _():
        inverse = lax.rsqrt(jnp.sum(squares[...], axis=0) + 1e-06)
        for m in range(3):
            store_split(half, m, 0.5 * ortho[m])
            store_split(scaled, m, ortho[m] * (factors[m] * inverse[m : m + 1]))
        for m, share, out in ((0, sq, bq), (1, sk, bk), (2, sv, bv)):
            out[...] = share[...] * inverse[m : m + 1]
        new(1, slice(2048, 2176), wk[...], mk, out_k)
        new(2, slice(2176, 2304), wv[...], mv, out_v)

    span = pl.ds(pl.multiple_of(step * WIDTH, WIDTH), WIDTH)
    new(0, span, wq[:, span], mq, out_q)


WIDTH = 2048 // STEPS
WIDE_SPECS = [column_spec(512), full_spec((512, RANK)), full_spec((512, RANK))]
WIDE_OUT = [
    jax.ShapeDtypeStruct((512, 2048), BF16),
    jax.ShapeDtypeStruct((512, RANK), BF16),
    jax.ShapeDtypeStruct((512, RANK), BF16),
]


def updates(factors, high, low, weights, ortho, rh, rl, squares, shares):
    share_specs = [full_spec((64, RANK)), full_spec((4, RANK)), full_spec((4, RANK))]
    return pl.pallas_call(
        functools.partial(update_kernel, factors),
        grid=(STEPS,),
        in_specs=[VMEM] * 12,
        out_specs=WIDE_SPECS + WIDE_SPECS + share_specs,
        out_shape=WIDE_OUT + WIDE_OUT + [jax.ShapeDtypeStruct(s.block_shape, F32) for s in share_specs],
        scratch_shapes=[pltpu.VMEM((3, 512, 2 * RANK), BF16)] * 2,
        compiler_params=pltpu.CompilerParams(vmem_limit_bytes=VMEM_LIMIT),
        cost_estimate=pl.CostEstimate(
            flops=12 * 512 * 2304 * RANK, bytes_accessed=16_000_000, transcendentals=0
        ),
        name="updates",
    )(high, low, *weights, ortho, rh, rl, squares, *shares)


def body(
    weight_q,
    momentum_q,
    grad_q,
    basis_q,
    weight_k,
    momentum_k,
    grad_k,
    basis_k,
    weight_v,
    momentum_v,
    grad_v,
    basis_v,
):
    weights = (weight_q, weight_k, weight_v)
    moments = (momentum_q, momentum_k, momentum_v)
    grads = (grad_q, grad_k, grad_v)
    factors = [
        0.25 * math.sqrt(w.shape[0] * lax.axis_size("fsdp") * w.shape[1] * lax.axis_size("tensor") / RANK)
        for w in weights
    ]

    high, low = blend_terms(moments, grads)
    mine = plane_gather(jnp.concatenate([basis_q, basis_k, basis_v], axis=0))
    mine, high, low = lax.optimization_barrier((mine, high, low))
    chunks = partial_rows(high, low, mine, swap_core(mine))
    own = small_kernel(total_kernel, (192, RANK), "own_rows", tensor_exchange(chunks))
    rows = [own] + [tensor_shift(own, d) for d in range(1, 8)]
    keep, send, projected = right_parts(high, low, rows)

    paired = small_kernel(pair_kernel, (HALF, RANK, RANK), "pair_sum", keep, swap_core(send))
    share = plane_exchange(paired.reshape(16, 88, RANK))
    share = small_kernel(repeat_total_kernel, (16, 88, RANK), "own_share", share)
    mine = plane_exchange(share).reshape(HALF, RANK, RANK)
    ortho, rh, rl, squares, *shares = factor_and_rotate(mine, swap_core(mine), projected)
    squares = tensor_exchange(squares)
    out = updates(factors, high, low, weights, ortho, rh, rl, squares, shares)
    return tuple(out[3 * j + i] for i in range(3) for j in (1, 0, 2))


def solution(mesh):
    placed = (
        P("fsdp", "tensor"),
        P("fsdp", "tensor"),
        P("fsdp", "tensor"),
        P(("tensor", "fsdp"), None),
    ) * 3
    return jax.shard_map(
        body,
        mesh=mesh,
        in_specs=placed,
        out_specs=(
            P("fsdp", "tensor"),
            P("fsdp", "tensor"),
            P(("tensor", "fsdp"), None),
        )
        * 3,
        check_vma=False,
    )
```

```python
import functools
import math

import jax
import jax.numpy as jnp
from jax import lax
from jax.experimental import pallas as pl
from jax.experimental.pallas import tpu as pltpu
from jax.sharding import PartitionSpec as P

RANK = 128
HIGHEST = lax.Precision.HIGHEST
F32 = jnp.float32
BF16 = jnp.bfloat16
PLANE = [[2 * i + c for i in range(16)] for c in range(2)]
SIBLING = [(i, i ^ 1) for i in range(32)]
STEPS = 4
BLOCKS = 22
HALF = BLOCKS // 2
VMEM_LIMIT = 24 * 1024 * 1024


def swap_core(x):
    return lax.ppermute(x, "fsdp", SIBLING)


def plane_exchange(x):
    return lax.all_to_all(x, "fsdp", 0, 0, tiled=True, axis_index_groups=PLANE)


def tensor_exchange(x):
    return lax.all_to_all(x, "tensor", 0, 0, tiled=True)


def dot(a, b, contract=(1, 0)):
    dims = (((contract[0],), (contract[1],)), ((), ()))
    return lax.dot_general(a, b, dims, preferred_element_type=F32)


def split(x):
    high = x.astype(BF16)
    return high, (x - high.astype(F32)).astype(BF16)


def blend_of(moment_ref, grad_ref):
    return moment_ref[...].astype(F32) + grad_ref[...].astype(F32)


def full_spec(shape):
    return pl.BlockSpec(shape, lambda i: (0,) * len(shape))


def column_spec(rows):
    return pl.BlockSpec((rows, 2048 // STEPS), lambda i: (0, i))


VMEM = pl.BlockSpec(memory_space=pltpu.VMEM)


def blend_kernel(mq, gq, mk, gk, mv, gv, high, low):
    for at, moment, grad in ((0, mq, gq), (2048, mk, gk), (2048 + RANK, mv, gv)):
        h, l = split(moment[...].astype(F32) + grad[...].astype(F32))
        span = slice(at, at + h.shape[1])
        high[:, span] = h
        low[:, span] = l


def blend_terms(moments, grads):
    def rows(width):
        return pl.BlockSpec((128, width), lambda i: (i, 0))

    return pl.pallas_call(
        blend_kernel,
        grid=(4,),
        in_specs=[rows(2048)] * 2 + [rows(RANK)] * 4,
        out_specs=[rows(2304)] * 2,
        out_shape=[jax.ShapeDtypeStruct((512, 2304), BF16)] * 2,
        compiler_params=pltpu.CompilerParams(vmem_limit_bytes=VMEM_LIMIT),
        cost_estimate=pl.CostEstimate(
            flops=4 * 512 * 2304, bytes_accessed=9_400_000, transcendentals=0
        ),
        name="blend_terms",
    )(*(x for group in zip(moments, grads) for x in group))


def small_kernel(kernel, shape, name, *operands):
    return pl.pallas_call(
        kernel,
        in_specs=[VMEM] * len(operands),
        out_specs=VMEM,
        out_shape=jax.ShapeDtypeStruct(shape, F32),
        compiler_params=pltpu.CompilerParams(vmem_limit_bytes=VMEM_LIMIT),
        name=name,
    )(*operands)


def repeat_bases_kernel(q, k, v, out):
    for i in range(out.shape[0]):
        out[i, :64] = q[...]
        out[i, 64:68] = k[...]
        out[i, 68:72] = v[...]


def repeat_bases(bases):
    return pl.pallas_call(
        repeat_bases_kernel,
        in_specs=[VMEM] * 3,
        out_specs=VMEM,
        out_shape=jax.ShapeDtypeStruct((16, 72, RANK), F32),
        name="repeat_bases",
    )(*bases)


def repeat_total_kernel(parts, out):
    total = jnp.sum(parts[...], axis=0)
    for i in range(out.shape[0]):
        out[i] = total


def pair_kernel(a, b, out):
    out[...] = a[...] + b[...]


def rows_kernel(high, low, mine, other, out, basis, small):
    first = lax.rem(lax.axis_index("fsdp"), 2) == 0
    for i in range(16):
        a, b = mine[i], other[i]
        pair = (jnp.where(first, a, b), jnp.where(first, b, a))
        for c in range(2):
            at = 128 * i + 64 * c
            qh, ql = split(pair[c][:64])
            basis[at : at + 64, :RANK] = qh
            basis[at : at + 64, RANK:] = ql
        for n in range(2):
            piece = [x[64 + 4 * n : 68 + 4 * n] for x in pair]
            small[n, 8 * i : 8 * i + 8] = jnp.concatenate(piece, axis=0)
    for n in range(2):
        qh, ql = split(small[n])
        basis[2048 + RANK * n : 2048 + RANK * n + RANK, :RANK] = qh
        basis[2048 + RANK * n : 2048 + RANK * n + RANK, RANK:] = ql
    for m, (lo, hi) in enumerate(((0, 2048), (2048, 2176), (2176, 2304))):
        for half in range(2):
            at = slice(256 * half, 256 * half + 256)
            both = dot(high[at, lo:hi], basis[lo:hi])
            rows = both[:, :RANK] + both[:, RANK:] + dot(low[at, lo:hi], basis[lo:hi, :RANK])
            for d in range(4):
                out[4 * half + d, 64 * m : 64 * m + 64] = rows[64 * d : 64 * d + 64]


def partial_rows(high, low, mine, other):
    return pl.pallas_call(
        rows_kernel,
        in_specs=[VMEM] * 4,
        out_specs=VMEM,
        out_shape=jax.ShapeDtypeStruct((8, 192, RANK), F32),
        scratch_shapes=[pltpu.VMEM((2304, 2 * RANK), BF16), pltpu.VMEM((2, RANK, RANK), F32)],
        compiler_params=pltpu.CompilerParams(vmem_limit_bytes=VMEM_LIMIT),
        cost_estimate=pl.CostEstimate(
            flops=6 * 512 * 2304 * RANK, bytes_accessed=7_000_000, transcendentals=0
        ),
        name="partial_rows",
    )(high, low, mine, other)


def half_of_right(half, high, low, projected, lhs, out):
    def times(m, lo, hi):
        both = dot(lhs[m], high[:, lo:hi])
        return both[:RANK] + both[RANK:] + dot(lhs[m, :RANK], low[:, lo:hi])

    first = 0 if half == 0 else HALF
    for lo in range(first, min(first + HALF, 16), 4):
        hi = min(lo + 4, first + HALF, 16)
        right = times(0, RANK * lo, RANK * hi)
        for i in range(hi - lo):
            out[lo - first + i] = right[:, RANK * i : RANK * i + RANK]
    if half == 1:
        out[16 - HALF] = times(1, 2048, 2176)
        out[17 - HALF] = times(2, 2176, 2304)
        for m in range(3):
            p = projected[m]
            out[18 - HALF + m] = jnp.dot(p.T, p, precision=HIGHEST, preferred_element_type=F32)
        out[21 - HALF] = jnp.zeros((RANK, RANK), F32)


def send_kernel(high, low, rows, send, projected, lhs):
    for d in range(8):
        for m in range(3):
            projected[m, 64 * d : 64 * d + 64] = rows[d, 64 * m : 64 * m + 64]
    for m in range(3):
        h, l = split(projected[m].T)
        lhs[m, :RANK] = h
        lhs[m, RANK:] = l
    core = lax.rem(lax.axis_index("fsdp"), 2)
    for half in range(2):
        pl.when(core != half)(
            functools.partial(half_of_right, half, high, low, projected, lhs, send)
        )


def keep_kernel(high, low, projected, lhs, keep):
    core = lax.rem(lax.axis_index("fsdp"), 2)
    for half in range(2):
        pl.when(core == half)(
            functools.partial(half_of_right, half, high, low, projected, lhs, keep)
        )


HALF_SHAPE = jax.ShapeDtypeStruct((HALF, RANK, RANK), F32)
HALF_COST = pl.CostEstimate(
    flops=3 * 512 * 2304 * RANK, bytes_accessed=5_000_000, transcendentals=0
)


def part_to_send(high, low, rows):
    return pl.pallas_call(
        send_kernel,
        in_specs=[VMEM] * 3,
        out_specs=[VMEM] * 3,
        out_shape=[
            HALF_SHAPE,
            jax.ShapeDtypeStruct((3, 512, RANK), F32),
            jax.ShapeDtypeStruct((3, 2 * RANK, 512), BF16),
        ],
        compiler_params=pltpu.CompilerParams(vmem_limit_bytes=VMEM_LIMIT),
        cost_estimate=HALF_COST,
        name="part_to_send",
    )(high, low, rows)


def part_to_keep(high, low, projected, lhs):
    return pl.pallas_call(
        keep_kernel,
        in_specs=[VMEM] * 4,
        out_specs=VMEM,
        out_shape=HALF_SHAPE,
        compiler_params=pltpu.CompilerParams(vmem_limit_bytes=VMEM_LIMIT),
        cost_estimate=HALF_COST,
        name="part_to_keep",
    )(high, low, projected, lhs)


def invert(grams):
    sub = lax.broadcasted_iota(jnp.int32, (8, RANK), 0)
    lane = lax.broadcasted_iota(jnp.int32, (8, RANK), 1)
    count = len(grams)
    rows = [[g[8 * p : 8 * p + 8] for p in range(16)] for g in grams]
    done = [[] for _ in grams]
    for p in range(16):
        lo = 8 * p
        for m in range(count):
            panel = rows[m][p]
            cols = [jnp.broadcast_to(panel[:, lo + k : lo + k + 1], (8, RANK)) for k in range(8)]
            inverse = jnp.zeros((8, RANK), F32)
            for j in range(8):
                at = sub == j
                here = lane == lo + j
                root = lax.rsqrt(jnp.broadcast_to(cols[j][j : j + 1], (8, RANK)))
                scale = root * root
                row = jnp.where(here, 1.0, jnp.broadcast_to(panel[j : j + 1], (8, RANK)))
                inverse = jnp.where(at, row * root, inverse)
                row = row * scale
                panel = jnp.where(at, row, jnp.where(here, 0.0, panel) - cols[j] * row)
                for k in range(j + 1, 8):
                    entry = jnp.broadcast_to(cols[k][j : j + 1], (8, RANK)) * scale
                    cols[k] = jnp.where(at, entry, cols[k] - cols[j] * entry)
            done[m].append(jnp.where(lane <= sub + lo, inverse, 0.0))
            inside = (lane >= lo) & (lane < lo + 8)
            if p < 15:
                ahead = rows[m][p + 1]
                total = jnp.where(inside, 0.0, ahead)
                for k in range(8):
                    column = jnp.broadcast_to(ahead[:, lo + k : lo + k + 1], (8, RANK))
                    total -= column * jnp.broadcast_to(panel[k : k + 1], (8, RANK))
                rows[m][p + 1] = total
            if p < 14:
                rest = jnp.concatenate(rows[m][p + 2 :], axis=0)
                pieces = [panel]
                if lo > 0:
                    pieces = [jnp.zeros((lo, RANK), F32)] + pieces
                pieces = pieces + [jnp.zeros((RANK - lo - 8, RANK), F32)]
                product = jnp.dot(
                    rest, jnp.concatenate(pieces, axis=0), precision=HIGHEST, preferred_element_type=F32
                )
                for i in range(p + 2, 16):
                    rows[m][i] = jnp.where(inside, 0.0, rows[m][i]) - product[8 * (i - p - 2) : 8 * (i - p - 1)]
    return [jnp.concatenate(d, axis=0) for d in done]


def factor_kernel(
    mine, other, projected, ortho, right_high, right_low, squares, sq, sk, sv, turned
):
    fsdp = lax.axis_index("fsdp")
    core = lax.rem(fsdp, 2)

    def block(j):
        return jnp.where(core == j // HALF, mine[j % HALF], other[j % HALF])

    inverses = invert([block(18 + m) for m in range(3)])
    for m, blocks in enumerate((range(16), (16,), (17,))):
        ih, il = split(inverses[m])
        ph, plow = split(projected[m])
        ortho[m] = dot(ph, ih, (1, 1)) + dot(ph, il, (1, 1)) + dot(plow, ih, (1, 1))
        stacked = jnp.concatenate([ih, il], axis=0)
        total = jnp.zeros((RANK, RANK), F32)
        for j in blocks:
            zh, zl = split(block(j))
            both = dot(stacked, zh)
            right = both[:RANK] + both[RANK:] + dot(ih, zl)
            total += right * right
            high, low = split(right)
            right_high[:, RANK * j : RANK * j + RANK] = high
            right_low[:, RANK * j : RANK * j + RANK] = low
            if m == 0:
                @pl.when(lax.div(fsdp, 2) == j)
                def _():
                    turned[0] = right.T
            else:
                turned[m] = right.T
        sums = jnp.sum(total.T, axis=0, keepdims=True)
        for d in range(8):
            squares[d, m : m + 1, :] = sums
    for d in range(8):
        squares[d, 3:, :] = jnp.zeros((5, RANK), F32)
    odd = lax.rem(fsdp, 2)
    sq[...] = turned[0, pl.ds(pl.multiple_of(odd * 64, 64), 64)]
    for m, out in ((1, sk), (2, sv)):
        tile = turned[m, pl.ds(pl.multiple_of(lax.div(fsdp, 2) * 8, 8), 8)]
        out[...] = jnp.where(odd == 0, tile[:4], tile[4:])


def factor_and_rotate(mine, other, projected):
    return pl.pallas_call(
        factor_kernel,
        in_specs=[VMEM, VMEM, VMEM],
        out_specs=[VMEM] * 7,
        out_shape=[
            jax.ShapeDtypeStruct((3, 512, RANK), F32),
            jax.ShapeDtypeStruct((RANK, 2304), BF16),
            jax.ShapeDtypeStruct((RANK, 2304), BF16),
            jax.ShapeDtypeStruct((8, 8, RANK), F32),
            jax.ShapeDtypeStruct((64, RANK), F32),
            jax.ShapeDtypeStruct((4, RANK), F32),
            jax.ShapeDtypeStruct((4, RANK), F32),
        ],
        scratch_shapes=[pltpu.VMEM((3, RANK, RANK), F32)],
        compiler_params=pltpu.CompilerParams(vmem_limit_bytes=VMEM_LIMIT),
        name="factor_and_rotate",
    )(mine, other, projected)


def update_kernel(
    factors, high, low, wq, wk, wv, ortho, rh, rl, squares, sq, sk, sv,
    mq, mk, mv, out_q, out_k, out_v, bq, bk, bv, lhs,
):
    step = pl.program_id(0)

    def new(m, span, weight, moment_out, weight_out):
        right = rh[:, span]
        product = dot(lhs[m], jnp.concatenate([right, right], axis=0))
        product += dot(lhs[m, :, :RANK], rl[:, span])
        blend = high[:, span].astype(F32) + low[:, span].astype(F32)
        moment_out[...] = (blend - product[:512]).astype(BF16)
        weight_out[...] = (weight.astype(F32) - product[512:]).astype(BF16)

    @pl.when(step == 0)
    def _():
        inverse = lax.rsqrt(jnp.sum(squares[...], axis=0) + 1e-06)
        for m in range(3):
            scale = factors[m] * inverse[m : m + 1]
            for at, left in ((0, 0.5 * ortho[m]), (512, ortho[m] * scale)):
                h, l = split(left)
                lhs[m, at : at + 512, :RANK] = h
                lhs[m, at : at + 512, RANK:] = l
        for m, share, out in ((0, sq, bq), (1, sk, bk), (2, sv, bv)):
            out[...] = share[...] * inverse[m : m + 1]
        new(1, slice(2048, 2176), wk[...], mk, out_k)
        new(2, slice(2176, 2304), wv[...], mv, out_v)

    span = pl.ds(pl.multiple_of(step * WIDTH, WIDTH), WIDTH)
    new(0, span, wq[:, span], mq, out_q)


WIDTH = 2048 // STEPS
WIDE_SPECS = [column_spec(512), full_spec((512, RANK)), full_spec((512, RANK))]
WIDE_OUT = [
    jax.ShapeDtypeStruct((512, 2048), BF16),
    jax.ShapeDtypeStruct((512, RANK), BF16),
    jax.ShapeDtypeStruct((512, RANK), BF16),
]


def updates(factors, high, low, weights, ortho, rh, rl, squares, shares):
    share_specs = [full_spec((64, RANK)), full_spec((4, RANK)), full_spec((4, RANK))]
    return pl.pallas_call(
        functools.partial(update_kernel, factors),
        grid=(STEPS,),
        in_specs=[VMEM] * 12,
        out_specs=WIDE_SPECS + WIDE_SPECS + share_specs,
        out_shape=WIDE_OUT + WIDE_OUT + [jax.ShapeDtypeStruct(s.block_shape, F32) for s in share_specs],
        scratch_shapes=[pltpu.VMEM((3, 1024, 2 * RANK), BF16)],
        compiler_params=pltpu.CompilerParams(vmem_limit_bytes=VMEM_LIMIT),
        cost_estimate=pl.CostEstimate(
            flops=12 * 512 * 2304 * RANK, bytes_accessed=16_000_000, transcendentals=0
        ),
        name="updates",
    )(high, low, *weights, ortho, rh, rl, squares, *shares)


def body(
    weight_q,
    momentum_q,
    grad_q,
    basis_q,
    weight_k,
    momentum_k,
    grad_k,
    basis_k,
    weight_v,
    momentum_v,
    grad_v,
    basis_v,
):
    weights = (weight_q, weight_k, weight_v)
    moments = (momentum_q, momentum_k, momentum_v)
    grads = (grad_q, grad_k, grad_v)
    factors = [
        0.25 * math.sqrt(w.shape[0] * lax.axis_size("fsdp") * w.shape[1] * lax.axis_size("tensor") / RANK)
        for w in weights
    ]

    high, low = blend_terms(moments, grads)
    mine = plane_exchange(repeat_bases((basis_q, basis_k, basis_v)))
    mine, high, low = lax.optimization_barrier((mine, high, low))
    chunks = partial_rows(high, low, mine, swap_core(mine))
    own = small_kernel(repeat_total_kernel, chunks.shape, "own_rows", tensor_exchange(chunks))
    rows = tensor_exchange(own)
    send, projected, lhs = part_to_send(high, low, rows)
    sent = swap_core(send)
    keep = part_to_keep(high, low, projected, lhs)

    paired = small_kernel(pair_kernel, (HALF, RANK, RANK), "pair_sum", keep, sent)
    share = plane_exchange(paired.reshape(16, 88, RANK))
    share = small_kernel(repeat_total_kernel, (16, 88, RANK), "own_share", share)
    mine = plane_exchange(share).reshape(HALF, RANK, RANK)
    ortho, rh, rl, squares, *shares = factor_and_rotate(mine, swap_core(mine), projected)
    squares = tensor_exchange(squares)
    out = updates(factors, high, low, weights, ortho, rh, rl, squares, shares)
    return tuple(out[3 * j + i] for i in range(3) for j in (1, 0, 2))


def solution(mesh):
    placed = (
        P("fsdp", "tensor"),
        P("fsdp", "tensor"),
        P("fsdp", "tensor"),
        P(("tensor", "fsdp"), None),
    ) * 3
    return jax.shard_map(
        body,
        mesh=mesh,
        in_specs=placed,
        out_specs=(
            P("fsdp", "tensor"),
            P("fsdp", "tensor"),
            P(("tensor", "fsdp"), None),
        )
        * 3,
        check_vma=False,
    )
```

```python
import functools
import math

import jax
import jax.numpy as jnp
from jax import lax
from jax.experimental import pallas as pl
from jax.experimental.pallas import tpu as pltpu
from jax.sharding import PartitionSpec as P

RANK = 128
HIGHEST = lax.Precision.HIGHEST
F32 = jnp.float32
BF16 = jnp.bfloat16
PLANE = [[2 * i + c for i in range(16)] for c in range(2)]
SIBLING = [(i, i ^ 1) for i in range(32)]
STEPS = 2
HALF = 9
SUMMED = HALF + 2
VMEM_LIMIT = 24 * 1024 * 1024


def swap_core(x):
    return lax.ppermute(x, "fsdp", SIBLING)


def plane_exchange(x):
    return lax.all_to_all(x, "fsdp", 0, 0, tiled=True, axis_index_groups=PLANE)


def tensor_exchange(x):
    return lax.all_to_all(x, "tensor", 0, 0, tiled=True)


def dot(a, b, contract=(1, 0)):
    dims = (((contract[0],), (contract[1],)), ((), ()))
    return lax.dot_general(a, b, dims, preferred_element_type=F32)


def split(x):
    high = x.astype(BF16)
    return high, (x - high.astype(F32)).astype(BF16)


def blend_of(moment_ref, grad_ref):
    return moment_ref[...].astype(F32) + grad_ref[...].astype(F32)


def full_spec(shape):
    return pl.BlockSpec(shape, lambda i: (0,) * len(shape))


def column_spec(rows):
    return pl.BlockSpec((rows, 2048 // STEPS), lambda i: (0, i))


VMEM = pl.BlockSpec(memory_space=pltpu.VMEM)


def blend_kernel(mq, gq, mk, gk, mv, gv, high, low):
    for at, moment, grad in ((0, mq, gq), (2048, mk, gk), (2048 + RANK, mv, gv)):
        h, l = split(moment[...].astype(F32) + grad[...].astype(F32))
        span = slice(at, at + h.shape[1])
        high[:, span] = h
        low[:, span] = l


def blend_terms(moments, grads):
    def rows(width):
        return pl.BlockSpec((128, width), lambda i: (i, 0))

    return pl.pallas_call(
        blend_kernel,
        grid=(4,),
        in_specs=[rows(2048)] * 2 + [rows(RANK)] * 4,
        out_specs=[rows(2304)] * 2,
        out_shape=[jax.ShapeDtypeStruct((512, 2304), BF16)] * 2,
        compiler_params=pltpu.CompilerParams(vmem_limit_bytes=VMEM_LIMIT),
        cost_estimate=pl.CostEstimate(
            flops=4 * 512 * 2304, bytes_accessed=9_400_000, transcendentals=0
        ),
        name="blend_terms",
    )(*(x for group in zip(moments, grads) for x in group))


def small_kernel(kernel, shape, name, *operands):
    return pl.pallas_call(
        kernel,
        in_specs=[VMEM] * len(operands),
        out_specs=VMEM,
        out_shape=jax.ShapeDtypeStruct(shape, F32),
        compiler_params=pltpu.CompilerParams(vmem_limit_bytes=VMEM_LIMIT),
        name=name,
    )(*operands)


def repeat_kernel(block, out):
    for i in range(out.shape[0]):
        out[i] = block[...]


def repeat_total_kernel(parts, out):
    total = jnp.sum(parts[...], axis=0)
    for i in range(out.shape[0]):
        out[i] = total


def pair_kernel(a, b, out):
    out[...] = a[...] + b[...]


def rows_kernel(high, low, mine, other, out, basis, small):
    first = lax.rem(lax.axis_index("fsdp"), 2) == 0
    for i in range(16):
        a, b = mine[i], other[i]
        pair = (jnp.where(first, a, b), jnp.where(first, b, a))
        for c in range(2):
            at = 128 * i + 64 * c
            qh, ql = split(pair[c][:64])
            basis[at : at + 64, :RANK] = qh
            basis[at : at + 64, RANK:] = ql
        for n in range(2):
            piece = [x[64 + 4 * n : 68 + 4 * n] for x in pair]
            small[n, 8 * i : 8 * i + 8] = jnp.concatenate(piece, axis=0)
    for n in range(2):
        qh, ql = split(small[n])
        basis[2048 + RANK * n : 2048 + RANK * n + RANK, :RANK] = qh
        basis[2048 + RANK * n : 2048 + RANK * n + RANK, RANK:] = ql
    for m, (lo, hi) in enumerate(((0, 2048), (2048, 2176), (2176, 2304))):
        for half in range(2):
            at = slice(256 * half, 256 * half + 256)
            both = dot(high[at, lo:hi], basis[lo:hi])
            rows = both[:, :RANK] + both[:, RANK:] + dot(low[at, lo:hi], basis[lo:hi, :RANK])
            for d in range(4):
                out[4 * half + d, 64 * m : 64 * m + 64] = rows[64 * d : 64 * d + 64]


def partial_rows(high, low, mine, other):
    return pl.pallas_call(
        rows_kernel,
        in_specs=[VMEM] * 4,
        out_specs=VMEM,
        out_shape=jax.ShapeDtypeStruct((8, 192, RANK), F32),
        scratch_shapes=[pltpu.VMEM((2304, 2 * RANK), BF16), pltpu.VMEM((2, RANK, RANK), F32)],
        compiler_params=pltpu.CompilerParams(vmem_limit_bytes=VMEM_LIMIT),
        cost_estimate=pl.CostEstimate(
            flops=6 * 512 * 2304 * RANK, bytes_accessed=7_000_000, transcendentals=0
        ),
        name="partial_rows",
    )(high, low, mine, other)


def grid_of_indices():
    row = lax.broadcasted_iota(jnp.int32, (RANK, RANK), 0)
    return row, lax.broadcasted_iota(jnp.int32, (RANK, RANK), 1)


def pack_symmetric(a, b, c):
    row, col = grid_of_indices()
    diagonal = jnp.sum(jnp.where(row == col, b, 0.0), axis=0, keepdims=True)
    first = jnp.where(row >= col, a, b.T)
    upper = jnp.where((row == 0) & (col > 0), diagonal, 0.0)
    upper = jnp.where((row == 1) & (col == RANK - 1), b[:1, :1], upper)
    return first, jnp.where(row >= col, c, upper)


def unpack_symmetric(first, second):
    row, col = grid_of_indices()
    turned = first.T
    diagonal = jnp.where(col[:1] == 0, second[1:2, RANK - 1 :], second[:1])
    a = jnp.where(row >= col, first, turned)
    b = jnp.where(row < col, first, jnp.where(row > col, turned, diagonal))
    return a, b, jnp.where(row >= col, second, second.T)


def half_of_right(half, high, low, lhs, out):
    def times(m, lo, hi):
        both = dot(lhs[m], high[:, lo:hi])
        return both[:RANK] + both[RANK:] + dot(lhs[m, :RANK], low[:, lo:hi])

    first = HALF * half
    for lo in range(first, min(first + HALF, 16), 3):
        hi = min(lo + 3, first + HALF, 16)
        right = times(0, RANK * lo, RANK * hi)
        for i in range(hi - lo):
            out[lo - first + i] = right[:, RANK * i : RANK * i + RANK]
    if half == 1:
        out[16 - HALF] = times(1, 2048, 2176)
        out[17 - HALF] = times(2, 2176, 2304)


def send_kernel(high, low, rows, send, projected, lhs, grams):
    for d in range(8):
        for m in range(3):
            projected[m, 64 * d : 64 * d + 64] = rows[d, 64 * m : 64 * m + 64]
    squares = []
    for m in range(3):
        p = projected[m]
        turned = p.T
        h, l = split(turned)
        lhs[m, :RANK] = h
        lhs[m, RANK:] = l
        squares.append(jnp.dot(turned, p, precision=HIGHEST, preferred_element_type=F32))
    core = lax.rem(lax.axis_index("fsdp"), 2)
    for half in range(2):
        pl.when(core != half)(functools.partial(half_of_right, half, high, low, lhs, send))
    for i, block in enumerate(pack_symmetric(*squares)):
        send[HALF + i] = block
        grams[i] = block


def keep_kernel(high, low, lhs, grams, keep):
    core = lax.rem(lax.axis_index("fsdp"), 2)
    for half in range(2):
        pl.when(core == half)(functools.partial(half_of_right, half, high, low, lhs, keep))
    for i in range(2):
        keep[HALF + i] = grams[i]


HALF_SHAPE = jax.ShapeDtypeStruct((SUMMED, RANK, RANK), F32)
HALF_COST = pl.CostEstimate(
    flops=3 * 512 * 2304 * RANK, bytes_accessed=5_000_000, transcendentals=0
)


def part_to_send(high, low, rows):
    return pl.pallas_call(
        send_kernel,
        in_specs=[VMEM] * 3,
        out_specs=[VMEM] * 4,
        out_shape=[
            HALF_SHAPE,
            jax.ShapeDtypeStruct((3, 512, RANK), F32),
            jax.ShapeDtypeStruct((3, 2 * RANK, 512), BF16),
            jax.ShapeDtypeStruct((2, RANK, RANK), F32),
        ],
        compiler_params=pltpu.CompilerParams(vmem_limit_bytes=VMEM_LIMIT),
        cost_estimate=HALF_COST,
        name="part_to_send",
    )(high, low, rows)


def part_to_keep(high, low, lhs, grams):
    return pl.pallas_call(
        keep_kernel,
        in_specs=[VMEM] * 4,
        out_specs=VMEM,
        out_shape=HALF_SHAPE,
        compiler_params=pltpu.CompilerParams(vmem_limit_bytes=VMEM_LIMIT),
        cost_estimate=HALF_COST,
        name="part_to_keep",
    )(high, low, lhs, grams)


def invert(grams):
    sub = lax.broadcasted_iota(jnp.int32, (8, RANK), 0)
    lane = lax.broadcasted_iota(jnp.int32, (8, RANK), 1)
    count = len(grams)
    rows = [[g[8 * p : 8 * p + 8] for p in range(16)] for g in grams]
    done = [[] for _ in grams]
    for p in range(16):
        lo = 8 * p
        for m in range(count):
            panel = rows[m][p]
            cols = [jnp.broadcast_to(panel[:, lo + k : lo + k + 1], (8, RANK)) for k in range(8)]
            inverse = jnp.zeros((8, RANK), F32)
            for j in range(8):
                at = sub == j
                here = lane == lo + j
                root = lax.rsqrt(jnp.broadcast_to(cols[j][j : j + 1], (8, RANK)))
                scale = root * root
                row = jnp.where(here, 1.0, jnp.broadcast_to(panel[j : j + 1], (8, RANK)))
                inverse = jnp.where(at, row * root, inverse)
                row = row * scale
                panel = jnp.where(at, row, jnp.where(here, 0.0, panel) - cols[j] * row)
                for k in range(j + 1, 8):
                    entry = jnp.broadcast_to(cols[k][j : j + 1], (8, RANK)) * scale
                    cols[k] = jnp.where(at, entry, cols[k] - cols[j] * entry)
            done[m].append(jnp.where(lane <= sub + lo, inverse, 0.0))
            inside = (lane >= lo) & (lane < lo + 8)
            if p < 15:
                ahead = rows[m][p + 1]
                total = jnp.where(inside, 0.0, ahead)
                for k in range(8):
                    column = jnp.broadcast_to(ahead[:, lo + k : lo + k + 1], (8, RANK))
                    total -= column * jnp.broadcast_to(panel[k : k + 1], (8, RANK))
                rows[m][p + 1] = total
            if p < 14:
                rest = jnp.concatenate(rows[m][p + 2 :], axis=0)
                pieces = [panel]
                if lo > 0:
                    pieces = [jnp.zeros((lo, RANK), F32)] + pieces
                pieces = pieces + [jnp.zeros((RANK - lo - 8, RANK), F32)]
                product = jnp.dot(
                    rest, jnp.concatenate(pieces, axis=0), precision=HIGHEST, preferred_element_type=F32
                )
                for i in range(p + 2, 16):
                    rows[m][i] = jnp.where(inside, 0.0, rows[m][i]) - product[8 * (i - p - 2) : 8 * (i - p - 1)]
    return [jnp.concatenate(d, axis=0) for d in done]


def factor_kernel(mine, projected, inverses, ortho):
    for m, inverse in enumerate(invert(unpack_symmetric(mine[HALF], mine[HALF + 1]))):
        inverses[m] = inverse
        ih, il = split(inverse)
        ph, plow = split(projected[m])
        ortho[m] = dot(ph, ih, (1, 1)) + dot(ph, il, (1, 1)) + dot(plow, ih, (1, 1))


def factor(mine, projected):
    return pl.pallas_call(
        factor_kernel,
        in_specs=[VMEM] * 2,
        out_specs=[VMEM] * 2,
        out_shape=[
            jax.ShapeDtypeStruct((3, RANK, RANK), F32),
            jax.ShapeDtypeStruct((3, 512, RANK), F32),
        ],
        compiler_params=pltpu.CompilerParams(vmem_limit_bytes=VMEM_LIMIT),
        cost_estimate=pl.CostEstimate(
            flops=6_000_000_000, bytes_accessed=3_000_000, transcendentals=0
        ),
        name="factor",
    )(mine, projected)


def rotate_kernel(mine, other, inverses, right_high, right_low, squares, sq, sk, sv, turned):
    fsdp = lax.axis_index("fsdp")
    core = lax.rem(fsdp, 2)

    def block(j):
        return jnp.where(core == j // HALF, mine[j % HALF], other[j % HALF])

    groups = ((0, range(0, 4)), (0, range(4, 8)), (0, range(8, 12)), (0, range(12, 16)))
    terms = [split(inverses[m]) for m in range(3)]
    stacked = [jnp.concatenate(pair, axis=0) for pair in terms]
    totals = [jnp.zeros((RANK, RANK), F32)] * 3
    for m, blocks in groups + ((1, (16,)), (2, (17,))):
        zh, zl = split(jnp.concatenate([block(j) for j in blocks], axis=1))
        both = dot(stacked[m], zh)
        right = both[:RANK] + both[RANK:] + dot(terms[m][0], zl)
        span = slice(RANK * blocks[0], RANK * blocks[-1] + RANK)
        right_high[:, span], right_low[:, span] = split(right)
        for i, j in enumerate(blocks):
            piece = right[:, RANK * i : RANK * i + RANK]
            totals[m] += piece * piece
            turned[j] = piece
    for m in range(3):
        sums = jnp.sum(totals[m].T, axis=0, keepdims=True)
        for d in range(8):
            squares[d, m : m + 1, :] = sums
    for d in range(8):
        squares[d, 3:, :] = jnp.zeros((5, RANK), F32)
    turned[0] = turned[lax.div(fsdp, 2)].T
    turned[1] = turned[16].T
    turned[2] = turned[17].T
    odd = lax.rem(fsdp, 2)
    sq[...] = turned[0, pl.ds(pl.multiple_of(odd * 64, 64), 64)]
    for m, out in ((1, sk), (2, sv)):
        tile = turned[m, pl.ds(pl.multiple_of(lax.div(fsdp, 2) * 8, 8), 8)]
        out[...] = jnp.where(odd == 0, tile[:4], tile[4:])


def rotate(mine, other, inverses):
    return pl.pallas_call(
        rotate_kernel,
        in_specs=[VMEM] * 3,
        out_specs=[VMEM] * 6,
        out_shape=[
            jax.ShapeDtypeStruct((RANK, 2304), BF16),
            jax.ShapeDtypeStruct((RANK, 2304), BF16),
            jax.ShapeDtypeStruct((8, 8, RANK), F32),
            jax.ShapeDtypeStruct((64, RANK), F32),
            jax.ShapeDtypeStruct((4, RANK), F32),
            jax.ShapeDtypeStruct((4, RANK), F32),
        ],
        scratch_shapes=[pltpu.VMEM((18, RANK, RANK), F32)],
        compiler_params=pltpu.CompilerParams(vmem_limit_bytes=VMEM_LIMIT),
        name="rotate",
    )(mine, other, inverses)


def update_kernel(
    factors, high, low, wq, wk, wv, ortho, rh, rl, squares, sq, sk, sv,
    mq, mk, mv, out_q, out_k, out_v, bq, bk, bv, lhs,
):
    step = pl.program_id(0)

    def new(m, span, weight, moment_out, weight_out):
        right = jnp.concatenate([rh[:, span], rh[:, span]], axis=0)
        low_right = rl[:, span]

        def product(at):
            return dot(lhs[m, at : at + 256], right) + dot(lhs[m, at : at + 256, :RANK], low_right)

        for at in (0, 256):
            part = slice(at, at + 256)
            blend = high[part, span].astype(F32) + low[part, span].astype(F32)
            moment_out[part] = (blend - product(at)).astype(BF16)
            weight_out[part] = (weight[part].astype(F32) - product(512 + at)).astype(BF16)

    @pl.when(step == 0)
    def _():
        inverse = lax.rsqrt(jnp.sum(squares[...], axis=0) + 1e-06)
        for m in range(3):
            scale = factors[m] * inverse[m : m + 1]
            for at, left in ((0, 0.5 * ortho[m]), (512, ortho[m] * scale)):
                h, l = split(left)
                lhs[m, at : at + 512, :RANK] = h
                lhs[m, at : at + 512, RANK:] = l
        for m, share, out in ((0, sq, bq), (1, sk, bk), (2, sv, bv)):
            out[...] = share[...] * inverse[m : m + 1]
        new(1, slice(2048, 2176), wk[...], mk, out_k)
        new(2, slice(2176, 2304), wv[...], mv, out_v)

    span = pl.ds(pl.multiple_of(step * WIDTH, WIDTH), WIDTH)
    new(0, span, wq[:, span], mq, out_q)


WIDTH = 2048 // STEPS
WIDE_SPECS = [column_spec(512), full_spec((512, RANK)), full_spec((512, RANK))]
WIDE_OUT = [
    jax.ShapeDtypeStruct((512, 2048), BF16),
    jax.ShapeDtypeStruct((512, RANK), BF16),
    jax.ShapeDtypeStruct((512, RANK), BF16),
]


def updates(factors, high, low, weights, ortho, rh, rl, squares, shares):
    share_specs = [full_spec((64, RANK)), full_spec((4, RANK)), full_spec((4, RANK))]
    return pl.pallas_call(
        functools.partial(update_kernel, factors),
        grid=(STEPS,),
        in_specs=[VMEM] * 12,
        out_specs=WIDE_SPECS + WIDE_SPECS + share_specs,
        out_shape=WIDE_OUT + WIDE_OUT + [jax.ShapeDtypeStruct(s.block_shape, F32) for s in share_specs],
        scratch_shapes=[pltpu.VMEM((3, 1024, 2 * RANK), BF16)],
        compiler_params=pltpu.CompilerParams(vmem_limit_bytes=VMEM_LIMIT),
        cost_estimate=pl.CostEstimate(
            flops=12 * 512 * 2304 * RANK, bytes_accessed=16_000_000, transcendentals=0
        ),
        name="updates",
    )(high, low, *weights, ortho, rh, rl, squares, *shares)


def body(
    weight_q,
    momentum_q,
    grad_q,
    basis_q,
    weight_k,
    momentum_k,
    grad_k,
    basis_k,
    weight_v,
    momentum_v,
    grad_v,
    basis_v,
):
    weights = (weight_q, weight_k, weight_v)
    moments = (momentum_q, momentum_k, momentum_v)
    grads = (grad_q, grad_k, grad_v)
    factors = [
        0.25 * math.sqrt(w.shape[0] * lax.axis_size("fsdp") * w.shape[1] * lax.axis_size("tensor") / RANK)
        for w in weights
    ]

    high, low = blend_terms(moments, grads)
    bases = jnp.concatenate([basis_q, basis_k, basis_v], axis=0)
    bases = small_kernel(repeat_kernel, (16,) + bases.shape, "repeat_bases", bases)
    mine = plane_exchange(bases)
    mine, high, low = lax.optimization_barrier((mine, high, low))
    chunks = partial_rows(high, low, mine, swap_core(mine))
    own = small_kernel(repeat_total_kernel, chunks.shape, "own_rows", tensor_exchange(chunks))
    rows = tensor_exchange(own)
    send, projected, lhs, grams = part_to_send(high, low, rows)
    sent = swap_core(send)
    keep = part_to_keep(high, low, lhs, grams)

    paired = small_kernel(pair_kernel, send.shape, "pair_sum", keep, sent)
    share = plane_exchange(paired.reshape(16, 88, RANK))
    share = small_kernel(repeat_total_kernel, (16, 88, RANK), "own_share", share)
    mine = plane_exchange(share).reshape(send.shape)
    other = swap_core(mine)
    inverses, ortho = factor(mine, projected)
    rh, rl, squares, *shares = rotate(mine, other, inverses)
    squares = tensor_exchange(squares)
    out = updates(factors, high, low, weights, ortho, rh, rl, squares, shares)
    return tuple(out[3 * j + i] for i in range(3) for j in (1, 0, 2))


def solution(mesh):
    placed = (
        P("fsdp", "tensor"),
        P("fsdp", "tensor"),
        P("fsdp", "tensor"),
        P(("tensor", "fsdp"), None),
    ) * 3
    return jax.shard_map(
        body,
        mesh=mesh,
        in_specs=placed,
        out_specs=(
            P("fsdp", "tensor"),
            P("fsdp", "tensor"),
            P(("tensor", "fsdp"), None),
        )
        * 3,
        check_vma=False,
    )
```

```python
import functools
import math

import jax
import jax.numpy as jnp
from jax import lax
from jax.experimental import pallas as pl
from jax.experimental.pallas import tpu as pltpu
from jax.sharding import PartitionSpec as P

RANK = 128
HIGHEST = lax.Precision.HIGHEST
F32 = jnp.float32
BF16 = jnp.bfloat16
PLANE = [[2 * i + c for i in range(16)] for c in range(2)]
SIBLING = [(i, i ^ 1) for i in range(32)]
STEPS = 2
HALF = 9
SUMMED = HALF + 2
VMEM_LIMIT = 24 * 1024 * 1024
EARLY_LIMIT = 60 * 1024 * 1024
BLEND_LIMIT = 50 * 1024 * 1024


def swap_core(x):
    return lax.ppermute(x, "fsdp", SIBLING)


def plane_exchange(x):
    return lax.all_to_all(x, "fsdp", 0, 0, tiled=True, axis_index_groups=PLANE)


def tensor_exchange(x):
    return lax.all_to_all(x, "tensor", 0, 0, tiled=True)


def dot(a, b, contract=(1, 0)):
    dims = (((contract[0],), (contract[1],)), ((), ()))
    return lax.dot_general(a, b, dims, preferred_element_type=F32)


def split(x):
    high = x.astype(BF16)
    return high, (x - high.astype(F32)).astype(BF16)


def blend_of(moment_ref, grad_ref):
    return moment_ref[...].astype(F32) + grad_ref[...].astype(F32)


def full_spec(shape):
    return pl.BlockSpec(shape, lambda i: (0,) * len(shape))


def column_spec(rows):
    return pl.BlockSpec((rows, 2048 // STEPS), lambda i: (0, i))


VMEM = pl.BlockSpec(memory_space=pltpu.VMEM)


SPLITS = ((0, 2048), (2048, 2176), (2176, 2304))
TERMS = [jax.ShapeDtypeStruct((512, 2304), BF16)] * 2


def early_blend_kernel(
    mq, gq, mk, gk, mv, gv, high_out, low_out, moments, grads, high, low, sems, out_sems
):
    @pl.when(lax.rem(lax.axis_index("fsdp"), 2) == 0)
    def _():
        fetches = []
        for i, ((lo, hi), moment, grad) in enumerate(zip(SPLITS, (mq, mk, mv), (gq, gk, gv))):
            fetches.append(pltpu.make_async_copy(moment, moments.at[:, lo:hi], sems.at[i, 0]))
            fetches.append(pltpu.make_async_copy(grad, grads.at[:, lo:hi], sems.at[i, 1]))
        for copy in fetches:
            copy.start()
        for copy in fetches:
            copy.wait()
        for at in range(0, 512, 64):
            part = slice(at, at + 64)
            high[part], low[part] = split(moments[part].astype(F32) + grads[part].astype(F32))
        stores = [
            pltpu.make_async_copy(high, high_out, out_sems.at[0]),
            pltpu.make_async_copy(low, low_out, out_sems.at[1]),
        ]
        for copy in stores:
            copy.start()
        for copy in stores:
            copy.wait()


def early_blend_terms(moments, grads):
    anywhere = pl.BlockSpec(memory_space=pl.ANY)
    return pl.pallas_call(
        early_blend_kernel,
        in_specs=[anywhere] * 6,
        out_specs=[anywhere] * 2,
        out_shape=TERMS,
        scratch_shapes=[pltpu.VMEM((512, 2304), BF16)] * 4
        + [pltpu.SemaphoreType.DMA((3, 2)), pltpu.SemaphoreType.DMA((2,))],
        compiler_params=pltpu.CompilerParams(vmem_limit_bytes=EARLY_LIMIT),
        name="early_blend_terms",
    )(*(x for group in zip(moments, grads) for x in group))


def blend_kernel(mq, gq, mk, gk, mv, gv, early_high, early_low, high, low):
    core = lax.rem(lax.axis_index("fsdp"), 2)

    @pl.when(core == 0)
    def _():
        high[...] = early_high[...]
        low[...] = early_low[...]

    @pl.when(core == 1)
    def _():
        for (lo, hi), moment, grad in zip(SPLITS, (mq, mk, mv), (gq, gk, gv)):
            blend = moment[...].astype(F32) + grad[...].astype(F32)
            high[:, lo:hi], low[:, lo:hi] = split(blend)


def blend_terms(moments, grads, early):
    def rows(width):
        return pl.BlockSpec((128, width), lambda i: (i, 0))

    return pl.pallas_call(
        blend_kernel,
        grid=(4,),
        in_specs=[rows(2048)] * 2 + [rows(RANK)] * 4 + [rows(2304)] * 2,
        out_specs=[rows(2304)] * 2,
        out_shape=TERMS,
        compiler_params=pltpu.CompilerParams(vmem_limit_bytes=BLEND_LIMIT),
        cost_estimate=pl.CostEstimate(
            flops=4 * 512 * 2304, bytes_accessed=14_000_000, transcendentals=0
        ),
        name="blend_terms",
    )(*(x for group in zip(moments, grads) for x in group), *early)


def small_kernel(kernel, shape, name, *operands):
    return pl.pallas_call(
        kernel,
        in_specs=[VMEM] * len(operands),
        out_specs=VMEM,
        out_shape=jax.ShapeDtypeStruct(shape, F32),
        compiler_params=pltpu.CompilerParams(vmem_limit_bytes=VMEM_LIMIT),
        name=name,
    )(*operands)


def repeat_kernel(own, sibling, out):
    first = lax.rem(lax.axis_index("fsdp"), 2) == 0
    a, b = own[...], sibling[...]
    low, high = jnp.where(first, a, b), jnp.where(first, b, a)
    for i in range(out.shape[0]):
        out[i, :72] = low
        out[i, 72:] = high


def repeat_total_kernel(parts, out):
    total = jnp.sum(parts[...], axis=0)
    for i in range(out.shape[0]):
        out[i] = total


def pair_kernel(a, b, out):
    out[...] = a[...] + b[...]


def rows_kernel(high, low, gathered, out, basis, small):
    for i in range(16):
        pair = (gathered[i, :72], gathered[i, 72:])
        for c in range(2):
            at = 128 * i + 64 * c
            qh, ql = split(pair[c][:64])
            basis[at : at + 64, :RANK] = qh
            basis[at : at + 64, RANK:] = ql
        for n in range(2):
            piece = [x[64 + 4 * n : 68 + 4 * n] for x in pair]
            small[n, 8 * i : 8 * i + 8] = jnp.concatenate(piece, axis=0)
    for n in range(2):
        qh, ql = split(small[n])
        basis[2048 + RANK * n : 2048 + RANK * n + RANK, :RANK] = qh
        basis[2048 + RANK * n : 2048 + RANK * n + RANK, RANK:] = ql
    for m, (lo, hi) in enumerate(((0, 2048), (2048, 2176), (2176, 2304))):
        for half in range(2):
            at = slice(256 * half, 256 * half + 256)
            both = dot(high[at, lo:hi], basis[lo:hi])
            rows = both[:, :RANK] + both[:, RANK:] + dot(low[at, lo:hi], basis[lo:hi, :RANK])
            for d in range(4):
                out[4 * half + d, 64 * m : 64 * m + 64] = rows[64 * d : 64 * d + 64]


def partial_rows(high, low, gathered):
    return pl.pallas_call(
        rows_kernel,
        in_specs=[VMEM] * 3,
        out_specs=VMEM,
        out_shape=jax.ShapeDtypeStruct((8, 192, RANK), F32),
        scratch_shapes=[pltpu.VMEM((2304, 2 * RANK), BF16), pltpu.VMEM((2, RANK, RANK), F32)],
        compiler_params=pltpu.CompilerParams(vmem_limit_bytes=VMEM_LIMIT),
        cost_estimate=pl.CostEstimate(
            flops=6 * 512 * 2304 * RANK, bytes_accessed=7_000_000, transcendentals=0
        ),
        name="partial_rows",
    )(high, low, gathered)


def grid_of_indices():
    row = lax.broadcasted_iota(jnp.int32, (RANK, RANK), 0)
    return row, lax.broadcasted_iota(jnp.int32, (RANK, RANK), 1)


def pack_symmetric(a, b, c):
    row, col = grid_of_indices()
    diagonal = jnp.sum(jnp.where(row == col, b, 0.0), axis=0, keepdims=True)
    first = jnp.where(row >= col, a, b.T)
    upper = jnp.where((row == 0) & (col > 0), diagonal, 0.0)
    upper = jnp.where((row == 1) & (col == RANK - 1), b[:1, :1], upper)
    return first, jnp.where(row >= col, c, upper)


def unpack_symmetric(first, second):
    row, col = grid_of_indices()
    turned = first.T
    diagonal = jnp.where(col[:1] == 0, second[1:2, RANK - 1 :], second[:1])
    a = jnp.where(row >= col, first, turned)
    b = jnp.where(row < col, first, jnp.where(row > col, turned, diagonal))
    return a, b, jnp.where(row >= col, second, second.T)


def half_of_right(half, high, low, lhs, out):
    def times(m, lo, hi):
        both = dot(lhs[m], high[:, lo:hi])
        return both[:RANK] + both[RANK:] + dot(lhs[m, :RANK], low[:, lo:hi])

    first = HALF * half
    for lo in range(first, min(first + HALF, 16), 3):
        hi = min(lo + 3, first + HALF, 16)
        right = times(0, RANK * lo, RANK * hi)
        for i in range(hi - lo):
            out[lo - first + i] = right[:, RANK * i : RANK * i + RANK]
    if half == 1:
        out[16 - HALF] = times(1, 2048, 2176)
        out[17 - HALF] = times(2, 2176, 2304)


def send_kernel(high, low, rows, send, projected, lhs, grams):
    for d in range(8):
        for m in range(3):
            projected[m, 64 * d : 64 * d + 64] = rows[d, 64 * m : 64 * m + 64]
    squares = []
    for m in range(3):
        p = projected[m]
        turned = p.T
        h, l = split(turned)
        lhs[m, :RANK] = h
        lhs[m, RANK:] = l
        squares.append(jnp.dot(turned, p, precision=HIGHEST, preferred_element_type=F32))
    core = lax.rem(lax.axis_index("fsdp"), 2)
    for half in range(2):
        pl.when(core != half)(functools.partial(half_of_right, half, high, low, lhs, send))
    for i, block in enumerate(pack_symmetric(*squares)):
        send[HALF + i] = block
        grams[i] = block


def keep_kernel(high, low, lhs, grams, keep):
    core = lax.rem(lax.axis_index("fsdp"), 2)
    for half in range(2):
        pl.when(core == half)(functools.partial(half_of_right, half, high, low, lhs, keep))
    for i in range(2):
        keep[HALF + i] = grams[i]


HALF_SHAPE = jax.ShapeDtypeStruct((SUMMED, RANK, RANK), F32)
HALF_COST = pl.CostEstimate(
    flops=3 * 512 * 2304 * RANK, bytes_accessed=5_000_000, transcendentals=0
)


def part_to_send(high, low, rows):
    return pl.pallas_call(
        send_kernel,
        in_specs=[VMEM] * 3,
        out_specs=[VMEM] * 4,
        out_shape=[
            HALF_SHAPE,
            jax.ShapeDtypeStruct((3, 512, RANK), F32),
            jax.ShapeDtypeStruct((3, 2 * RANK, 512), BF16),
            jax.ShapeDtypeStruct((2, RANK, RANK), F32),
        ],
        compiler_params=pltpu.CompilerParams(vmem_limit_bytes=VMEM_LIMIT),
        cost_estimate=HALF_COST,
        name="part_to_send",
    )(high, low, rows)


def part_to_keep(high, low, lhs, grams):
    return pl.pallas_call(
        keep_kernel,
        in_specs=[VMEM] * 4,
        out_specs=VMEM,
        out_shape=HALF_SHAPE,
        compiler_params=pltpu.CompilerParams(vmem_limit_bytes=VMEM_LIMIT),
        cost_estimate=HALF_COST,
        name="part_to_keep",
    )(high, low, lhs, grams)


def invert(grams):
    sub = lax.broadcasted_iota(jnp.int32, (8, RANK), 0)
    lane = lax.broadcasted_iota(jnp.int32, (8, RANK), 1)
    count = len(grams)
    rows = [[g[8 * p : 8 * p + 8] for p in range(16)] for g in grams]
    done = [[] for _ in grams]
    for p in range(16):
        lo = 8 * p
        for m in range(count):
            panel = rows[m][p]
            cols = [jnp.broadcast_to(panel[:, lo + k : lo + k + 1], (8, RANK)) for k in range(8)]
            inverse = jnp.zeros((8, RANK), F32)
            for j in range(8):
                at = sub == j
                here = lane == lo + j
                root = lax.rsqrt(jnp.broadcast_to(cols[j][j : j + 1], (8, RANK)))
                scale = root * root
                row = jnp.where(here, 1.0, jnp.broadcast_to(panel[j : j + 1], (8, RANK)))
                inverse = jnp.where(at, row * root, inverse)
                row = row * scale
                panel = jnp.where(at, row, jnp.where(here, 0.0, panel) - cols[j] * row)
                for k in range(j + 1, 8):
                    entry = jnp.broadcast_to(cols[k][j : j + 1], (8, RANK)) * scale
                    cols[k] = jnp.where(at, entry, cols[k] - cols[j] * entry)
            done[m].append(jnp.where(lane <= sub + lo, inverse, 0.0))
            inside = (lane >= lo) & (lane < lo + 8)
            if p < 15:
                ahead = rows[m][p + 1]
                total = jnp.where(inside, 0.0, ahead)
                for k in range(8):
                    column = jnp.broadcast_to(ahead[:, lo + k : lo + k + 1], (8, RANK))
                    total -= column * jnp.broadcast_to(panel[k : k + 1], (8, RANK))
                rows[m][p + 1] = total
            if p < 14:
                rest = jnp.concatenate(rows[m][p + 2 :], axis=0)
                pieces = [panel]
                if lo > 0:
                    pieces = [jnp.zeros((lo, RANK), F32)] + pieces
                pieces = pieces + [jnp.zeros((RANK - lo - 8, RANK), F32)]
                product = jnp.dot(
                    rest, jnp.concatenate(pieces, axis=0), precision=HIGHEST, preferred_element_type=F32
                )
                for i in range(p + 2, 16):
                    rows[m][i] = jnp.where(inside, 0.0, rows[m][i]) - product[8 * (i - p - 2) : 8 * (i - p - 1)]
    return [jnp.concatenate(d, axis=0) for d in done]


def factor_kernel(mine, projected, inverses, ortho):
    for m, inverse in enumerate(invert(unpack_symmetric(mine[HALF], mine[HALF + 1]))):
        inverses[m] = inverse
        ih, il = split(inverse)
        ph, plow = split(projected[m])
        ortho[m] = dot(ph, ih, (1, 1)) + dot(ph, il, (1, 1)) + dot(plow, ih, (1, 1))


def factor(mine, projected):
    return pl.pallas_call(
        factor_kernel,
        in_specs=[VMEM] * 2,
        out_specs=[VMEM] * 2,
        out_shape=[
            jax.ShapeDtypeStruct((3, RANK, RANK), F32),
            jax.ShapeDtypeStruct((3, 512, RANK), F32),
        ],
        compiler_params=pltpu.CompilerParams(vmem_limit_bytes=VMEM_LIMIT),
        cost_estimate=pl.CostEstimate(
            flops=6_000_000_000, bytes_accessed=3_000_000, transcendentals=0
        ),
        name="factor",
    )(mine, projected)


def rotate_kernel(mine, other, inverses, right_high, right_low, squares, sq, sk, sv, turned):
    fsdp = lax.axis_index("fsdp")
    core = lax.rem(fsdp, 2)

    def block(j):
        return jnp.where(core == j // HALF, mine[j % HALF], other[j % HALF])

    groups = ((0, range(0, 4)), (0, range(4, 8)), (0, range(8, 12)), (0, range(12, 16)))
    terms = [split(inverses[m]) for m in range(3)]
    stacked = [jnp.concatenate(pair, axis=0) for pair in terms]
    totals = [jnp.zeros((RANK, RANK), F32)] * 3
    for m, blocks in groups + ((1, (16,)), (2, (17,))):
        zh, zl = split(jnp.concatenate([block(j) for j in blocks], axis=1))
        both = dot(stacked[m], zh)
        right = both[:RANK] + both[RANK:] + dot(terms[m][0], zl)
        span = slice(RANK * blocks[0], RANK * blocks[-1] + RANK)
        right_high[:, span], right_low[:, span] = split(right)
        for i, j in enumerate(blocks):
            piece = right[:, RANK * i : RANK * i + RANK]
            totals[m] += piece * piece
            turned[j] = piece
    for m in range(3):
        sums = jnp.sum(totals[m].T, axis=0, keepdims=True)
        for d in range(8):
            squares[d, m : m + 1, :] = sums
    for d in range(8):
        squares[d, 3:, :] = jnp.zeros((5, RANK), F32)
    turned[0] = turned[lax.div(fsdp, 2)].T
    turned[1] = turned[16].T
    turned[2] = turned[17].T
    odd = lax.rem(fsdp, 2)
    sq[...] = turned[0, pl.ds(pl.multiple_of(odd * 64, 64), 64)]
    for m, out in ((1, sk), (2, sv)):
        tile = turned[m, pl.ds(pl.multiple_of(lax.div(fsdp, 2) * 8, 8), 8)]
        out[...] = jnp.where(odd == 0, tile[:4], tile[4:])


def rotate(mine, other, inverses):
    return pl.pallas_call(
        rotate_kernel,
        in_specs=[VMEM] * 3,
        out_specs=[VMEM] * 6,
        out_shape=[
            jax.ShapeDtypeStruct((RANK, 2304), BF16),
            jax.ShapeDtypeStruct((RANK, 2304), BF16),
            jax.ShapeDtypeStruct((8, 8, RANK), F32),
            jax.ShapeDtypeStruct((64, RANK), F32),
            jax.ShapeDtypeStruct((4, RANK), F32),
            jax.ShapeDtypeStruct((4, RANK), F32),
        ],
        scratch_shapes=[pltpu.VMEM((18, RANK, RANK), F32)],
        compiler_params=pltpu.CompilerParams(vmem_limit_bytes=VMEM_LIMIT),
        name="rotate",
    )(mine, other, inverses)


def update_kernel(
    factors, high, low, wq, wk, wv, ortho, rh, rl, squares, sq, sk, sv,
    mq, mk, mv, out_q, out_k, out_v, bq, bk, bv, lhs,
):
    step = pl.program_id(0)

    def new(m, span, weight, moment_out, weight_out):
        right = jnp.concatenate([rh[:, span], rh[:, span]], axis=0)
        low_right = rl[:, span]

        def product(at):
            return dot(lhs[m, at : at + 256], right) + dot(lhs[m, at : at + 256, :RANK], low_right)

        for at in (0, 256):
            part = slice(at, at + 256)
            blend = high[part, span].astype(F32) + low[part, span].astype(F32)
            moment_out[part] = (blend - product(at)).astype(BF16)
            weight_out[part] = (weight[part].astype(F32) - product(512 + at)).astype(BF16)

    @pl.when(step == 0)
    def _():
        inverse = lax.rsqrt(jnp.sum(squares[...], axis=0) + 1e-06)
        for m in range(3):
            scale = factors[m] * inverse[m : m + 1]
            for at, left in ((0, 0.5 * ortho[m]), (512, ortho[m] * scale)):
                h, l = split(left)
                lhs[m, at : at + 512, :RANK] = h
                lhs[m, at : at + 512, RANK:] = l
        for m, share, out in ((0, sq, bq), (1, sk, bk), (2, sv, bv)):
            out[...] = share[...] * inverse[m : m + 1]
        new(1, slice(2048, 2176), wk[...], mk, out_k)
        new(2, slice(2176, 2304), wv[...], mv, out_v)

    span = pl.ds(pl.multiple_of(step * WIDTH, WIDTH), WIDTH)
    new(0, span, wq[:, span], mq, out_q)


WIDTH = 2048 // STEPS
WIDE_SPECS = [column_spec(512), full_spec((512, RANK)), full_spec((512, RANK))]
WIDE_OUT = [
    jax.ShapeDtypeStruct((512, 2048), BF16),
    jax.ShapeDtypeStruct((512, RANK), BF16),
    jax.ShapeDtypeStruct((512, RANK), BF16),
]


def updates(factors, high, low, weights, ortho, rh, rl, squares, shares):
    share_specs = [full_spec((64, RANK)), full_spec((4, RANK)), full_spec((4, RANK))]
    return pl.pallas_call(
        functools.partial(update_kernel, factors),
        grid=(STEPS,),
        in_specs=[VMEM] * 12,
        out_specs=WIDE_SPECS + WIDE_SPECS + share_specs,
        out_shape=WIDE_OUT + WIDE_OUT + [jax.ShapeDtypeStruct(s.block_shape, F32) for s in share_specs],
        scratch_shapes=[pltpu.VMEM((3, 1024, 2 * RANK), BF16)],
        compiler_params=pltpu.CompilerParams(vmem_limit_bytes=VMEM_LIMIT),
        cost_estimate=pl.CostEstimate(
            flops=12 * 512 * 2304 * RANK, bytes_accessed=16_000_000, transcendentals=0
        ),
        name="updates",
    )(high, low, *weights, ortho, rh, rl, squares, *shares)


def body(
    weight_q,
    momentum_q,
    grad_q,
    basis_q,
    weight_k,
    momentum_k,
    grad_k,
    basis_k,
    weight_v,
    momentum_v,
    grad_v,
    basis_v,
):
    weights = (weight_q, weight_k, weight_v)
    moments = (momentum_q, momentum_k, momentum_v)
    grads = (grad_q, grad_k, grad_v)
    factors = [
        0.25 * math.sqrt(w.shape[0] * lax.axis_size("fsdp") * w.shape[1] * lax.axis_size("tensor") / RANK)
        for w in weights
    ]

    bases = jnp.concatenate([basis_q, basis_k, basis_v], axis=0)
    sibling, momentum_q = lax.optimization_barrier((swap_core(bases), momentum_q))
    early = early_blend_terms((momentum_q, momentum_k, momentum_v), grads)
    bases = small_kernel(repeat_kernel, (16, 144, RANK), "repeat_bases", bases, sibling)
    bases, early = lax.optimization_barrier((bases, early))
    gathered = plane_exchange(bases)
    high, low = blend_terms(moments, grads, early)
    gathered, high, low = lax.optimization_barrier((gathered, high, low))
    chunks = partial_rows(high, low, gathered)
    own = small_kernel(repeat_total_kernel, chunks.shape, "own_rows", tensor_exchange(chunks))
    rows = tensor_exchange(own)
    send, projected, lhs, grams = part_to_send(high, low, rows)
    sent = swap_core(send)
    keep = part_to_keep(high, low, lhs, grams)

    paired = small_kernel(pair_kernel, send.shape, "pair_sum", keep, sent)
    share = plane_exchange(paired.reshape(16, 88, RANK))
    share = small_kernel(repeat_total_kernel, (16, 88, RANK), "own_share", share)
    mine = plane_exchange(share).reshape(send.shape)
    other = swap_core(mine)
    inverses, ortho = factor(mine, projected)
    rh, rl, squares, *shares = rotate(mine, other, inverses)
    squares = tensor_exchange(squares)
    out = updates(factors, high, low, weights, ortho, rh, rl, squares, shares)
    return tuple(out[3 * j + i] for i in range(3) for j in (1, 0, 2))


def solution(mesh):
    placed = (
        P("fsdp", "tensor"),
        P("fsdp", "tensor"),
        P("fsdp", "tensor"),
        P(("tensor", "fsdp"), None),
    ) * 3
    return jax.shard_map(
        body,
        mesh=mesh,
        in_specs=placed,
        out_specs=(
            P("fsdp", "tensor"),
            P("fsdp", "tensor"),
            P(("tensor", "fsdp"), None),
        )
        * 3,
        check_vma=False,
    )
```

```python
import functools
import math

import jax
import jax.numpy as jnp
from jax import lax
from jax.experimental import pallas as pl
from jax.experimental.pallas import tpu as pltpu
from jax.sharding import PartitionSpec as P

RANK = 128
HIGHEST = lax.Precision.HIGHEST
F32 = jnp.float32
BF16 = jnp.bfloat16
PLANE = [[2 * i + c for i in range(16)] for c in range(2)]
SIBLING = [(i, i ^ 1) for i in range(32)]
STEPS = 2
HALF = 9
SUMMED = HALF + 2
VMEM_LIMIT = 24 * 1024 * 1024
EARLY_LIMIT = 60 * 1024 * 1024
BLEND_LIMIT = 46 * 1024 * 1024


def swap_core(x):
    return lax.ppermute(x, "fsdp", SIBLING)


def plane_exchange(x):
    return lax.all_to_all(x, "fsdp", 0, 0, tiled=True, axis_index_groups=PLANE)


def tensor_exchange(x):
    return lax.all_to_all(x, "tensor", 0, 0, tiled=True)


def dot(a, b, contract=(1, 0)):
    dims = (((contract[0],), (contract[1],)), ((), ()))
    return lax.dot_general(a, b, dims, preferred_element_type=F32)


def split(x):
    high = x.astype(BF16)
    return high, (x - high.astype(F32)).astype(BF16)


def blend_of(moment_ref, grad_ref):
    return moment_ref[...].astype(F32) + grad_ref[...].astype(F32)


def full_spec(shape):
    return pl.BlockSpec(shape, lambda i: (0,) * len(shape))


def column_spec(rows):
    return pl.BlockSpec((rows, 2048 // STEPS), lambda i: (0, i))


VMEM = pl.BlockSpec(memory_space=pltpu.VMEM)


SPLITS = ((0, 2048), (2048, 2176), (2176, 2304))
TERMS = [jax.ShapeDtypeStruct((512, 2304), BF16)] * 2


def early_blend_kernel(
    mq, gq, mk, gk, mv, gv, high_out, low_out, moments, grads, high, low, sems, out_sems
):
    @pl.when(lax.rem(lax.axis_index("fsdp"), 2) == 0)
    def _():
        fetches = []
        for i, ((lo, hi), moment, grad) in enumerate(zip(SPLITS, (mq, mk, mv), (gq, gk, gv))):
            fetches.append(pltpu.make_async_copy(moment, moments.at[:, lo:hi], sems.at[i, 0]))
            fetches.append(pltpu.make_async_copy(grad, grads.at[:, lo:hi], sems.at[i, 1]))
        for copy in fetches:
            copy.start()
        for copy in fetches:
            copy.wait()
        for at in range(0, 512, 64):
            part = slice(at, at + 64)
            high[part], low[part] = split(moments[part].astype(F32) + grads[part].astype(F32))
        stores = [
            pltpu.make_async_copy(high, high_out, out_sems.at[0]),
            pltpu.make_async_copy(low, low_out, out_sems.at[1]),
        ]
        for copy in stores:
            copy.start()
        for copy in stores:
            copy.wait()


def early_blend_terms(moments, grads):
    anywhere = pl.BlockSpec(memory_space=pl.ANY)
    return pl.pallas_call(
        early_blend_kernel,
        in_specs=[anywhere] * 6,
        out_specs=[anywhere] * 2,
        out_shape=TERMS,
        scratch_shapes=[pltpu.VMEM((512, 2304), BF16)] * 4
        + [pltpu.SemaphoreType.DMA((3, 2)), pltpu.SemaphoreType.DMA((2,))],
        compiler_params=pltpu.CompilerParams(vmem_limit_bytes=EARLY_LIMIT),
        name="early_blend_terms",
    )(*(x for group in zip(moments, grads) for x in group))


def blend_kernel(mq, gq, mk, gk, mv, gv, early_high, early_low, high, low, sems):
    core = lax.rem(lax.axis_index("fsdp"), 2)

    @pl.when(core == 0)
    def _():
        copies = [
            pltpu.make_async_copy(early_high, high, sems.at[0]),
            pltpu.make_async_copy(early_low, low, sems.at[1]),
        ]
        for copy in copies:
            copy.start()
        for copy in copies:
            copy.wait()

    @pl.when(core == 1)
    def _():
        for (lo, hi), moment, grad in zip(SPLITS, (mq, mk, mv), (gq, gk, gv)):
            for at in range(0, 512, 64):
                part = slice(at, at + 64)
                blend = moment[part].astype(F32) + grad[part].astype(F32)
                high[part, lo:hi], low[part, lo:hi] = split(blend)


def blend_terms(moments, grads, early):
    return pl.pallas_call(
        blend_kernel,
        in_specs=[VMEM] * 6 + [pl.BlockSpec(memory_space=pl.ANY)] * 2,
        out_specs=[VMEM] * 2,
        out_shape=TERMS,
        scratch_shapes=[pltpu.SemaphoreType.DMA((2,))],
        compiler_params=pltpu.CompilerParams(vmem_limit_bytes=BLEND_LIMIT),
        cost_estimate=pl.CostEstimate(
            flops=4 * 512 * 2304, bytes_accessed=14_000_000, transcendentals=0
        ),
        name="blend_terms",
    )(*(x for group in zip(moments, grads) for x in group), *early)


def small_kernel(kernel, shape, name, *operands):
    return pl.pallas_call(
        kernel,
        in_specs=[VMEM] * len(operands),
        out_specs=VMEM,
        out_shape=jax.ShapeDtypeStruct(shape, F32),
        compiler_params=pltpu.CompilerParams(vmem_limit_bytes=VMEM_LIMIT),
        name=name,
    )(*operands)


def repeat_kernel(own, sibling, out):
    first = lax.rem(lax.axis_index("fsdp"), 2) == 0
    a, b = own[...], sibling[...]
    low, high = jnp.where(first, a, b), jnp.where(first, b, a)
    for i in range(out.shape[0]):
        out[i, :72] = low
        out[i, 72:] = high


def repeat_total_kernel(parts, out):
    total = jnp.sum(parts[...], axis=0)
    for i in range(out.shape[0]):
        out[i] = total


def pair_kernel(a, b, out):
    out[...] = a[...] + b[...]


def rows_kernel(high, low, gathered, out, basis, small):
    for i in range(16):
        pair = (gathered[i, :72], gathered[i, 72:])
        for c in range(2):
            at = 128 * i + 64 * c
            qh, ql = split(pair[c][:64])
            basis[at : at + 64, :RANK] = qh
            basis[at : at + 64, RANK:] = ql
        for n in range(2):
            piece = [x[64 + 4 * n : 68 + 4 * n] for x in pair]
            small[n, 8 * i : 8 * i + 8] = jnp.concatenate(piece, axis=0)
    for n in range(2):
        qh, ql = split(small[n])
        basis[2048 + RANK * n : 2048 + RANK * n + RANK, :RANK] = qh
        basis[2048 + RANK * n : 2048 + RANK * n + RANK, RANK:] = ql
    for m, (lo, hi) in enumerate(((0, 2048), (2048, 2176), (2176, 2304))):
        for half in range(2):
            at = slice(256 * half, 256 * half + 256)
            both = dot(high[at, lo:hi], basis[lo:hi])
            rows = both[:, :RANK] + both[:, RANK:] + dot(low[at, lo:hi], basis[lo:hi, :RANK])
            for d in range(4):
                out[4 * half + d, 64 * m : 64 * m + 64] = rows[64 * d : 64 * d + 64]


def partial_rows(high, low, gathered):
    return pl.pallas_call(
        rows_kernel,
        in_specs=[VMEM] * 3,
        out_specs=VMEM,
        out_shape=jax.ShapeDtypeStruct((8, 192, RANK), F32),
        scratch_shapes=[pltpu.VMEM((2304, 2 * RANK), BF16), pltpu.VMEM((2, RANK, RANK), F32)],
        compiler_params=pltpu.CompilerParams(vmem_limit_bytes=VMEM_LIMIT),
        cost_estimate=pl.CostEstimate(
            flops=6 * 512 * 2304 * RANK, bytes_accessed=7_000_000, transcendentals=0
        ),
        name="partial_rows",
    )(high, low, gathered)


def grid_of_indices():
    row = lax.broadcasted_iota(jnp.int32, (RANK, RANK), 0)
    return row, lax.broadcasted_iota(jnp.int32, (RANK, RANK), 1)


def pack_symmetric(a, b, c):
    row, col = grid_of_indices()
    diagonal = jnp.sum(jnp.where(row == col, b, 0.0), axis=0, keepdims=True)
    first = jnp.where(row >= col, a, b.T)
    upper = jnp.where((row == 0) & (col > 0), diagonal, 0.0)
    upper = jnp.where((row == 1) & (col == RANK - 1), b[:1, :1], upper)
    return first, jnp.where(row >= col, c, upper)


def unpack_symmetric(first, second):
    row, col = grid_of_indices()
    turned = first.T
    diagonal = jnp.where(col[:1] == 0, second[1:2, RANK - 1 :], second[:1])
    a = jnp.where(row >= col, first, turned)
    b = jnp.where(row < col, first, jnp.where(row > col, turned, diagonal))
    return a, b, jnp.where(row >= col, second, second.T)


def half_of_right(half, high, low, lhs, out):
    def times(m, lo, hi):
        both = dot(lhs[m], high[:, lo:hi])
        return both[:RANK] + both[RANK:] + dot(lhs[m, :RANK], low[:, lo:hi])

    first = HALF * half
    for lo in range(first, min(first + HALF, 16), 3):
        hi = min(lo + 3, first + HALF, 16)
        right = times(0, RANK * lo, RANK * hi)
        for i in range(hi - lo):
            out[lo - first + i] = right[:, RANK * i : RANK * i + RANK]
    if half == 1:
        out[16 - HALF] = times(1, 2048, 2176)
        out[17 - HALF] = times(2, 2176, 2304)


def send_kernel(high, low, rows, send, projected, lhs, grams):
    for d in range(8):
        for m in range(3):
            projected[m, 64 * d : 64 * d + 64] = rows[d, 64 * m : 64 * m + 64]
    squares = []
    for m in range(3):
        p = projected[m]
        turned = p.T
        h, l = split(turned)
        lhs[m, :RANK] = h
        lhs[m, RANK:] = l
        squares.append(jnp.dot(turned, p, precision=HIGHEST, preferred_element_type=F32))
    core = lax.rem(lax.axis_index("fsdp"), 2)
    for half in range(2):
        pl.when(core != half)(functools.partial(half_of_right, half, high, low, lhs, send))
    for i, block in enumerate(pack_symmetric(*squares)):
        send[HALF + i] = block
        grams[i] = block


def keep_kernel(high, low, lhs, grams, keep):
    core = lax.rem(lax.axis_index("fsdp"), 2)
    for half in range(2):
        pl.when(core == half)(functools.partial(half_of_right, half, high, low, lhs, keep))
    for i in range(2):
        keep[HALF + i] = grams[i]


HALF_SHAPE = jax.ShapeDtypeStruct((SUMMED, RANK, RANK), F32)
HALF_COST = pl.CostEstimate(
    flops=3 * 512 * 2304 * RANK, bytes_accessed=5_000_000, transcendentals=0
)


def part_to_send(high, low, rows):
    return pl.pallas_call(
        send_kernel,
        in_specs=[VMEM] * 3,
        out_specs=[VMEM] * 4,
        out_shape=[
            HALF_SHAPE,
            jax.ShapeDtypeStruct((3, 512, RANK), F32),
            jax.ShapeDtypeStruct((3, 2 * RANK, 512), BF16),
            jax.ShapeDtypeStruct((2, RANK, RANK), F32),
        ],
        compiler_params=pltpu.CompilerParams(vmem_limit_bytes=VMEM_LIMIT),
        cost_estimate=HALF_COST,
        name="part_to_send",
    )(high, low, rows)


def part_to_keep(high, low, lhs, grams):
    return pl.pallas_call(
        keep_kernel,
        in_specs=[VMEM] * 4,
        out_specs=VMEM,
        out_shape=HALF_SHAPE,
        compiler_params=pltpu.CompilerParams(vmem_limit_bytes=VMEM_LIMIT),
        cost_estimate=HALF_COST,
        name="part_to_keep",
    )(high, low, lhs, grams)


def invert(grams):
    sub = lax.broadcasted_iota(jnp.int32, (8, RANK), 0)
    lane = lax.broadcasted_iota(jnp.int32, (8, RANK), 1)
    count = len(grams)
    rows = [[g[8 * p : 8 * p + 8] for p in range(16)] for g in grams]
    done = [[] for _ in grams]
    for p in range(16):
        lo = 8 * p
        for m in range(count):
            panel = rows[m][p]
            cols = [jnp.broadcast_to(panel[:, lo + k : lo + k + 1], (8, RANK)) for k in range(8)]
            inverse = jnp.zeros((8, RANK), F32)
            for j in range(8):
                at = sub == j
                here = lane == lo + j
                root = lax.rsqrt(jnp.broadcast_to(cols[j][j : j + 1], (8, RANK)))
                scale = root * root
                row = jnp.where(here, 1.0, jnp.broadcast_to(panel[j : j + 1], (8, RANK)))
                inverse = jnp.where(at, row * root, inverse)
                row = row * scale
                panel = jnp.where(at, row, jnp.where(here, 0.0, panel) - cols[j] * row)
                for k in range(j + 1, 8):
                    entry = jnp.broadcast_to(cols[k][j : j + 1], (8, RANK)) * scale
                    cols[k] = jnp.where(at, entry, cols[k] - cols[j] * entry)
            done[m].append(jnp.where(lane <= sub + lo, inverse, 0.0))
            inside = (lane >= lo) & (lane < lo + 8)
            if p < 15:
                ahead = rows[m][p + 1]
                total = jnp.where(inside, 0.0, ahead)
                for k in range(8):
                    column = jnp.broadcast_to(ahead[:, lo + k : lo + k + 1], (8, RANK))
                    total -= column * jnp.broadcast_to(panel[k : k + 1], (8, RANK))
                rows[m][p + 1] = total
            if p < 14:
                rest = jnp.concatenate(rows[m][p + 2 :], axis=0)
                pieces = [panel]
                if lo > 0:
                    pieces = [jnp.zeros((lo, RANK), F32)] + pieces
                pieces = pieces + [jnp.zeros((RANK - lo - 8, RANK), F32)]
                product = jnp.dot(
                    rest, jnp.concatenate(pieces, axis=0), precision=HIGHEST, preferred_element_type=F32
                )
                for i in range(p + 2, 16):
                    rows[m][i] = jnp.where(inside, 0.0, rows[m][i]) - product[8 * (i - p - 2) : 8 * (i - p - 1)]
    return [jnp.concatenate(d, axis=0) for d in done]


def factor_kernel(mine, projected, inverses, ortho):
    for m, inverse in enumerate(invert(unpack_symmetric(mine[HALF], mine[HALF + 1]))):
        inverses[m] = inverse
        ih, il = split(inverse)
        ph, plow = split(projected[m])
        ortho[m] = dot(ph, ih, (1, 1)) + dot(ph, il, (1, 1)) + dot(plow, ih, (1, 1))


def factor(mine, projected):
    return pl.pallas_call(
        factor_kernel,
        in_specs=[VMEM] * 2,
        out_specs=[VMEM] * 2,
        out_shape=[
            jax.ShapeDtypeStruct((3, RANK, RANK), F32),
            jax.ShapeDtypeStruct((3, 512, RANK), F32),
        ],
        compiler_params=pltpu.CompilerParams(vmem_limit_bytes=VMEM_LIMIT),
        cost_estimate=pl.CostEstimate(
            flops=6_000_000_000, bytes_accessed=3_000_000, transcendentals=0
        ),
        name="factor",
    )(mine, projected)


def rotate_kernel(mine, other, inverses, right_high, right_low, squares, sq, sk, sv, turned):
    fsdp = lax.axis_index("fsdp")
    core = lax.rem(fsdp, 2)

    def block(j):
        return jnp.where(core == j // HALF, mine[j % HALF], other[j % HALF])

    groups = ((0, range(0, 4)), (0, range(4, 8)), (0, range(8, 12)), (0, range(12, 16)))
    terms = [split(inverses[m]) for m in range(3)]
    stacked = [jnp.concatenate(pair, axis=0) for pair in terms]
    totals = [jnp.zeros((RANK, RANK), F32)] * 3
    for m, blocks in groups + ((1, (16,)), (2, (17,))):
        zh, zl = split(jnp.concatenate([block(j) for j in blocks], axis=1))
        both = dot(stacked[m], zh)
        right = both[:RANK] + both[RANK:] + dot(terms[m][0], zl)
        span = slice(RANK * blocks[0], RANK * blocks[-1] + RANK)
        right_high[:, span], right_low[:, span] = split(right)
        for i, j in enumerate(blocks):
            piece = right[:, RANK * i : RANK * i + RANK]
            totals[m] += piece * piece
            turned[j] = piece
    for m in range(3):
        sums = jnp.sum(totals[m].T, axis=0, keepdims=True)
        for d in range(8):
            squares[d, m : m + 1, :] = sums
    for d in range(8):
        squares[d, 3:, :] = jnp.zeros((5, RANK), F32)
    turned[0] = turned[lax.div(fsdp, 2)].T
    turned[1] = turned[16].T
    turned[2] = turned[17].T
    odd = lax.rem(fsdp, 2)
    sq[...] = turned[0, pl.ds(pl.multiple_of(odd * 64, 64), 64)]
    for m, out in ((1, sk), (2, sv)):
        tile = turned[m, pl.ds(pl.multiple_of(lax.div(fsdp, 2) * 8, 8), 8)]
        out[...] = jnp.where(odd == 0, tile[:4], tile[4:])


def rotate(mine, other, inverses):
    return pl.pallas_call(
        rotate_kernel,
        in_specs=[VMEM] * 3,
        out_specs=[VMEM] * 6,
        out_shape=[
            jax.ShapeDtypeStruct((RANK, 2304), BF16),
            jax.ShapeDtypeStruct((RANK, 2304), BF16),
            jax.ShapeDtypeStruct((8, 8, RANK), F32),
            jax.ShapeDtypeStruct((64, RANK), F32),
            jax.ShapeDtypeStruct((4, RANK), F32),
            jax.ShapeDtypeStruct((4, RANK), F32),
        ],
        scratch_shapes=[pltpu.VMEM((18, RANK, RANK), F32)],
        compiler_params=pltpu.CompilerParams(vmem_limit_bytes=VMEM_LIMIT),
        name="rotate",
    )(mine, other, inverses)


def update_kernel(
    factors, high, low, wq, wk, wv, ortho, rh, rl, squares, sq, sk, sv,
    mq, mk, mv, out_q, out_k, out_v, bq, bk, bv, lhs,
):
    step = pl.program_id(0)

    def new(m, span, weight, moment_out, weight_out):
        right = jnp.concatenate([rh[:, span], rh[:, span]], axis=0)
        low_right = rl[:, span]

        def product(at):
            return dot(lhs[m, at : at + 256], right) + dot(lhs[m, at : at + 256, :RANK], low_right)

        for at in (0, 256):
            part = slice(at, at + 256)
            blend = high[part, span].astype(F32) + low[part, span].astype(F32)
            moment_out[part] = (blend - product(at)).astype(BF16)
            weight_out[part] = (weight[part].astype(F32) - product(512 + at)).astype(BF16)

    @pl.when(step == 0)
    def _():
        inverse = lax.rsqrt(jnp.sum(squares[...], axis=0) + 1e-06)
        for m in range(3):
            scale = factors[m] * inverse[m : m + 1]
            for at, left in ((0, 0.5 * ortho[m]), (512, ortho[m] * scale)):
                h, l = split(left)
                lhs[m, at : at + 512, :RANK] = h
                lhs[m, at : at + 512, RANK:] = l
        for m, share, out in ((0, sq, bq), (1, sk, bk), (2, sv, bv)):
            out[...] = share[...] * inverse[m : m + 1]
        new(1, slice(2048, 2176), wk[...], mk, out_k)
        new(2, slice(2176, 2304), wv[...], mv, out_v)

    span = pl.ds(pl.multiple_of(step * WIDTH, WIDTH), WIDTH)
    new(0, span, wq[:, span], mq, out_q)


WIDTH = 2048 // STEPS
WIDE_SPECS = [column_spec(512), full_spec((512, RANK)), full_spec((512, RANK))]
WIDE_OUT = [
    jax.ShapeDtypeStruct((512, 2048), BF16),
    jax.ShapeDtypeStruct((512, RANK), BF16),
    jax.ShapeDtypeStruct((512, RANK), BF16),
]


def updates(factors, high, low, weights, ortho, rh, rl, squares, shares):
    share_specs = [full_spec((64, RANK)), full_spec((4, RANK)), full_spec((4, RANK))]
    return pl.pallas_call(
        functools.partial(update_kernel, factors),
        grid=(STEPS,),
        in_specs=[VMEM] * 12,
        out_specs=WIDE_SPECS + WIDE_SPECS + share_specs,
        out_shape=WIDE_OUT + WIDE_OUT + [jax.ShapeDtypeStruct(s.block_shape, F32) for s in share_specs],
        scratch_shapes=[pltpu.VMEM((3, 1024, 2 * RANK), BF16)],
        compiler_params=pltpu.CompilerParams(vmem_limit_bytes=VMEM_LIMIT),
        cost_estimate=pl.CostEstimate(
            flops=12 * 512 * 2304 * RANK, bytes_accessed=16_000_000, transcendentals=0
        ),
        name="updates",
    )(high, low, *weights, ortho, rh, rl, squares, *shares)


def body(
    weight_q,
    momentum_q,
    grad_q,
    basis_q,
    weight_k,
    momentum_k,
    grad_k,
    basis_k,
    weight_v,
    momentum_v,
    grad_v,
    basis_v,
):
    weights = (weight_q, weight_k, weight_v)
    moments = (momentum_q, momentum_k, momentum_v)
    grads = (grad_q, grad_k, grad_v)
    factors = [
        0.25 * math.sqrt(w.shape[0] * lax.axis_size("fsdp") * w.shape[1] * lax.axis_size("tensor") / RANK)
        for w in weights
    ]

    bases = jnp.concatenate([basis_q, basis_k, basis_v], axis=0)
    sibling, momentum_q = lax.optimization_barrier((swap_core(bases), momentum_q))
    early = early_blend_terms((momentum_q, momentum_k, momentum_v), grads)
    bases = small_kernel(repeat_kernel, (16, 144, RANK), "repeat_bases", bases, sibling)
    bases, early = lax.optimization_barrier((bases, early))
    gathered = plane_exchange(bases)
    high, low = blend_terms(moments, grads, early)
    gathered, high, low = lax.optimization_barrier((gathered, high, low))
    chunks = partial_rows(high, low, gathered)
    own = small_kernel(repeat_total_kernel, chunks.shape, "own_rows", tensor_exchange(chunks))
    rows = tensor_exchange(own)
    send, projected, lhs, grams = part_to_send(high, low, rows)
    sent = swap_core(send)
    keep = part_to_keep(high, low, lhs, grams)

    paired = small_kernel(pair_kernel, send.shape, "pair_sum", keep, sent)
    share = plane_exchange(paired.reshape(16, 88, RANK))
    share = small_kernel(repeat_total_kernel, (16, 88, RANK), "own_share", share)
    mine = plane_exchange(share).reshape(send.shape)
    other = swap_core(mine)
    inverses, ortho = factor(mine, projected)
    rh, rl, squares, *shares = rotate(mine, other, inverses)
    squares = tensor_exchange(squares)
    out = updates(factors, high, low, weights, ortho, rh, rl, squares, shares)
    return tuple(out[3 * j + i] for i in range(3) for j in (1, 0, 2))


def solution(mesh):
    placed = (
        P("fsdp", "tensor"),
        P("fsdp", "tensor"),
        P("fsdp", "tensor"),
        P(("tensor", "fsdp"), None),
    ) * 3
    return jax.shard_map(
        body,
        mesh=mesh,
        in_specs=placed,
        out_specs=(
            P("fsdp", "tensor"),
            P("fsdp", "tensor"),
            P(("tensor", "fsdp"), None),
        )
        * 3,
        check_vma=False,
    )
```

```python
import functools
import math

import jax
import jax.numpy as jnp
from jax import lax
from jax.experimental import pallas as pl
from jax.experimental.pallas import tpu as pltpu
from jax.sharding import PartitionSpec as P

RANK = 128
HIGHEST = lax.Precision.HIGHEST
F32 = jnp.float32
BF16 = jnp.bfloat16
PLANE = [[2 * i + c for i in range(16)] for c in range(2)]
SIBLING = [(i, i ^ 1) for i in range(32)]
STEPS = 2
HALF = 9
SUMMED = HALF + 2
VMEM_LIMIT = 24 * 1024 * 1024
EARLY_LIMIT = 60 * 1024 * 1024
BLEND_LIMIT = 46 * 1024 * 1024


def swap_core(x):
    return lax.ppermute(x, "fsdp", SIBLING)


def plane_exchange(x):
    return lax.all_to_all(x, "fsdp", 0, 0, tiled=True, axis_index_groups=PLANE)


def tensor_exchange(x):
    return lax.all_to_all(x, "tensor", 0, 0, tiled=True)


def dot(a, b, contract=(1, 0)):
    dims = (((contract[0],), (contract[1],)), ((), ()))
    return lax.dot_general(a, b, dims, preferred_element_type=F32)


def split(x):
    high = x.astype(BF16)
    return high, (x - high.astype(F32)).astype(BF16)


def blend_of(moment_ref, grad_ref):
    return moment_ref[...].astype(F32) + grad_ref[...].astype(F32)


def full_spec(shape):
    return pl.BlockSpec(shape, lambda i: (0,) * len(shape))


def column_spec(rows):
    return pl.BlockSpec((rows, 2048 // STEPS), lambda i: (0, i))


VMEM = pl.BlockSpec(memory_space=pltpu.VMEM)


SPLITS = ((0, 2048), (2048, 2176), (2176, 2304))
TERMS = [jax.ShapeDtypeStruct((512, 2304), BF16)] * 2


def early_blend_kernel(
    mq, gq, mk, gk, mv, gv, high_out, low_out, moments, grads, high, low, sems, out_sems
):
    @pl.when(lax.rem(lax.axis_index("fsdp"), 2) == 0)
    def _():
        fetches = []
        for i, ((lo, hi), moment, grad) in enumerate(zip(SPLITS, (mq, mk, mv), (gq, gk, gv))):
            fetches.append(pltpu.make_async_copy(moment, moments.at[:, lo:hi], sems.at[i, 0]))
            fetches.append(pltpu.make_async_copy(grad, grads.at[:, lo:hi], sems.at[i, 1]))
        for copy in fetches:
            copy.start()
        for copy in fetches:
            copy.wait()
        for at in range(0, 512, 64):
            part = slice(at, at + 64)
            high[part], low[part] = split(moments[part].astype(F32) + grads[part].astype(F32))
        stores = [
            pltpu.make_async_copy(high, high_out, out_sems.at[0]),
            pltpu.make_async_copy(low, low_out, out_sems.at[1]),
        ]
        for copy in stores:
            copy.start()
        for copy in stores:
            copy.wait()


def early_blend_terms(moments, grads):
    anywhere = pl.BlockSpec(memory_space=pl.ANY)
    return pl.pallas_call(
        early_blend_kernel,
        in_specs=[anywhere] * 6,
        out_specs=[anywhere] * 2,
        out_shape=TERMS,
        scratch_shapes=[pltpu.VMEM((512, 2304), BF16)] * 4
        + [pltpu.SemaphoreType.DMA((3, 2)), pltpu.SemaphoreType.DMA((2,))],
        compiler_params=pltpu.CompilerParams(vmem_limit_bytes=EARLY_LIMIT),
        name="early_blend_terms",
    )(*(x for group in zip(moments, grads) for x in group))


def blend_kernel(mq, gq, mk, gk, mv, gv, early_high, early_low, high, low, sems):
    core = lax.rem(lax.axis_index("fsdp"), 2)

    @pl.when(core == 0)
    def _():
        copies = [
            pltpu.make_async_copy(early_high, high, sems.at[0]),
            pltpu.make_async_copy(early_low, low, sems.at[1]),
        ]
        for copy in copies:
            copy.start()
        for copy in copies:
            copy.wait()

    @pl.when(core == 1)
    def _():
        for (lo, hi), moment, grad in zip(SPLITS, (mq, mk, mv), (gq, gk, gv)):
            for at in range(0, 512, 64):
                part = slice(at, at + 64)
                blend = moment[part].astype(F32) + grad[part].astype(F32)
                high[part, lo:hi], low[part, lo:hi] = split(blend)


def blend_terms(moments, grads, early):
    return pl.pallas_call(
        blend_kernel,
        in_specs=[VMEM] * 6 + [pl.BlockSpec(memory_space=pl.ANY)] * 2,
        out_specs=[VMEM] * 2,
        out_shape=TERMS,
        scratch_shapes=[pltpu.SemaphoreType.DMA((2,))],
        compiler_params=pltpu.CompilerParams(vmem_limit_bytes=BLEND_LIMIT),
        cost_estimate=pl.CostEstimate(
            flops=4 * 512 * 2304, bytes_accessed=14_000_000, transcendentals=0
        ),
        name="blend_terms",
    )(*(x for group in zip(moments, grads) for x in group), *early)


def small_kernel(kernel, shape, name, *operands):
    return pl.pallas_call(
        kernel,
        in_specs=[VMEM] * len(operands),
        out_specs=VMEM,
        out_shape=jax.ShapeDtypeStruct(shape, F32),
        compiler_params=pltpu.CompilerParams(vmem_limit_bytes=VMEM_LIMIT),
        name=name,
    )(*operands)


def repeat_kernel(own, sibling, out):
    first = lax.rem(lax.axis_index("fsdp"), 2) == 0
    a, b = own[...], sibling[...]
    low, high = jnp.where(first, a, b), jnp.where(first, b, a)
    for i in range(out.shape[0]):
        out[i, :72] = low
        out[i, 72:] = high


def repeat_total_kernel(parts, out):
    total = jnp.sum(parts[...], axis=0)
    for i in range(out.shape[0]):
        out[i] = total


def pair_kernel(a, b, out):
    out[...] = a[...] + b[...]


def high_rows_kernel(high, gathered, out, basis, small):
    for i in range(16):
        pair = (gathered[i, :72], gathered[i, 72:])
        for c in range(2):
            at = 128 * i + 64 * c
            qh, ql = split(pair[c][:64])
            basis[at : at + 64, :RANK] = qh
            basis[at : at + 64, RANK:] = ql
        for n in range(2):
            piece = [x[64 + 4 * n : 68 + 4 * n] for x in pair]
            small[n, 8 * i : 8 * i + 8] = jnp.concatenate(piece, axis=0)
    for n in range(2):
        qh, ql = split(small[n])
        basis[2048 + RANK * n : 2048 + RANK * n + RANK, :RANK] = qh
        basis[2048 + RANK * n : 2048 + RANK * n + RANK, RANK:] = ql
    for m, (lo, hi) in enumerate(SPLITS):
        for half in range(2):
            both = dot(high[256 * half : 256 * half + 256, lo:hi], basis[lo:hi])
            rows = both[:, :RANK] + both[:, RANK:]
            for d in range(4):
                out[4 * half + d, 64 * m : 64 * m + 64] = rows[64 * d : 64 * d + 64]


def low_rows_kernel(low, basis, part, out):
    for m, (lo, hi) in enumerate(SPLITS):
        for half in range(2):
            rows = dot(low[256 * half : 256 * half + 256, lo:hi], basis[lo:hi, :RANK])
            for d in range(4):
                at = (4 * half + d, slice(64 * m, 64 * m + 64))
                out[at] = part[at] + rows[64 * d : 64 * d + 64]


ROWS_SHAPE = jax.ShapeDtypeStruct((8, 192, RANK), F32)


def partial_rows(high, low, gathered):
    params = pltpu.CompilerParams(vmem_limit_bytes=VMEM_LIMIT)
    part, basis = pl.pallas_call(
        high_rows_kernel,
        in_specs=[VMEM] * 2,
        out_specs=[VMEM] * 2,
        out_shape=[ROWS_SHAPE, jax.ShapeDtypeStruct((2304, 2 * RANK), BF16)],
        scratch_shapes=[pltpu.VMEM((2, RANK, RANK), F32)],
        compiler_params=params,
        cost_estimate=pl.CostEstimate(
            flops=4 * 512 * 2304 * RANK, bytes_accessed=7_000_000, transcendentals=0
        ),
        name="high_rows",
    )(high, gathered)
    return pl.pallas_call(
        low_rows_kernel,
        in_specs=[VMEM] * 3,
        out_specs=VMEM,
        out_shape=ROWS_SHAPE,
        compiler_params=params,
        cost_estimate=pl.CostEstimate(
            flops=2 * 512 * 2304 * RANK, bytes_accessed=4_000_000, transcendentals=0
        ),
        name="low_rows",
    )(low, basis, part)


def grid_of_indices():
    row = lax.broadcasted_iota(jnp.int32, (RANK, RANK), 0)
    return row, lax.broadcasted_iota(jnp.int32, (RANK, RANK), 1)


def pack_symmetric(a, b, c):
    row, col = grid_of_indices()
    diagonal = jnp.sum(jnp.where(row == col, b, 0.0), axis=0, keepdims=True)
    first = jnp.where(row >= col, a, b.T)
    upper = jnp.where((row == 0) & (col > 0), diagonal, 0.0)
    upper = jnp.where((row == 1) & (col == RANK - 1), b[:1, :1], upper)
    return first, jnp.where(row >= col, c, upper)


def unpack_symmetric(first, second):
    row, col = grid_of_indices()
    turned = first.T
    diagonal = jnp.where(col[:1] == 0, second[1:2, RANK - 1 :], second[:1])
    a = jnp.where(row >= col, first, turned)
    b = jnp.where(row < col, first, jnp.where(row > col, turned, diagonal))
    return a, b, jnp.where(row >= col, second, second.T)


def half_of_right(half, high, low, lhs, out):
    def times(m, lo, hi):
        both = dot(lhs[m], high[:, lo:hi])
        return both[:RANK] + both[RANK:] + dot(lhs[m, :RANK], low[:, lo:hi])

    first = HALF * half
    for lo in range(first, min(first + HALF, 16), 3):
        hi = min(lo + 3, first + HALF, 16)
        right = times(0, RANK * lo, RANK * hi)
        for i in range(hi - lo):
            out[lo - first + i] = right[:, RANK * i : RANK * i + RANK]
    if half == 1:
        out[16 - HALF] = times(1, 2048, 2176)
        out[17 - HALF] = times(2, 2176, 2304)


def send_kernel(high, low, rows, send, projected, lhs, grams):
    for d in range(8):
        for m in range(3):
            projected[m, 64 * d : 64 * d + 64] = rows[d, 64 * m : 64 * m + 64]
    squares = []
    for m in range(3):
        p = projected[m]
        turned = p.T
        h, l = split(turned)
        lhs[m, :RANK] = h
        lhs[m, RANK:] = l
        squares.append(jnp.dot(turned, p, precision=HIGHEST, preferred_element_type=F32))
    core = lax.rem(lax.axis_index("fsdp"), 2)
    for half in range(2):
        pl.when(core != half)(functools.partial(half_of_right, half, high, low, lhs, send))
    for i, block in enumerate(pack_symmetric(*squares)):
        send[HALF + i] = block
        grams[i] = block


def keep_kernel(high, low, lhs, grams, keep):
    core = lax.rem(lax.axis_index("fsdp"), 2)
    for half in range(2):
        pl.when(core == half)(functools.partial(half_of_right, half, high, low, lhs, keep))
    for i in range(2):
        keep[HALF + i] = grams[i]


HALF_SHAPE = jax.ShapeDtypeStruct((SUMMED, RANK, RANK), F32)
HALF_COST = pl.CostEstimate(
    flops=3 * 512 * 2304 * RANK, bytes_accessed=5_000_000, transcendentals=0
)


def part_to_send(high, low, rows):
    return pl.pallas_call(
        send_kernel,
        in_specs=[VMEM] * 3,
        out_specs=[VMEM] * 4,
        out_shape=[
            HALF_SHAPE,
            jax.ShapeDtypeStruct((3, 512, RANK), F32),
            jax.ShapeDtypeStruct((3, 2 * RANK, 512), BF16),
            jax.ShapeDtypeStruct((2, RANK, RANK), F32),
        ],
        compiler_params=pltpu.CompilerParams(vmem_limit_bytes=VMEM_LIMIT),
        cost_estimate=HALF_COST,
        name="part_to_send",
    )(high, low, rows)


def part_to_keep(high, low, lhs, grams):
    return pl.pallas_call(
        keep_kernel,
        in_specs=[VMEM] * 4,
        out_specs=VMEM,
        out_shape=HALF_SHAPE,
        compiler_params=pltpu.CompilerParams(vmem_limit_bytes=VMEM_LIMIT),
        cost_estimate=HALF_COST,
        name="part_to_keep",
    )(high, low, lhs, grams)


def invert(grams):
    sub = lax.broadcasted_iota(jnp.int32, (8, RANK), 0)
    lane = lax.broadcasted_iota(jnp.int32, (8, RANK), 1)
    count = len(grams)
    rows = [[g[8 * p : 8 * p + 8] for p in range(16)] for g in grams]
    done = [[] for _ in grams]
    for p in range(16):
        lo = 8 * p
        for m in range(count):
            panel = rows[m][p]
            cols = [jnp.broadcast_to(panel[:, lo + k : lo + k + 1], (8, RANK)) for k in range(8)]
            inverse = jnp.zeros((8, RANK), F32)
            for j in range(8):
                at = sub == j
                here = lane == lo + j
                root = lax.rsqrt(jnp.broadcast_to(cols[j][j : j + 1], (8, RANK)))
                scale = root * root
                row = jnp.where(here, 1.0, jnp.broadcast_to(panel[j : j + 1], (8, RANK)))
                inverse = jnp.where(at, row * root, inverse)
                row = row * scale
                panel = jnp.where(at, row, jnp.where(here, 0.0, panel) - cols[j] * row)
                for k in range(j + 1, 8):
                    entry = jnp.broadcast_to(cols[k][j : j + 1], (8, RANK)) * scale
                    cols[k] = jnp.where(at, entry, cols[k] - cols[j] * entry)
            done[m].append(jnp.where(lane <= sub + lo, inverse, 0.0))
            inside = (lane >= lo) & (lane < lo + 8)
            if p < 15:
                ahead = rows[m][p + 1]
                total = jnp.where(inside, 0.0, ahead)
                for k in range(8):
                    column = jnp.broadcast_to(ahead[:, lo + k : lo + k + 1], (8, RANK))
                    total -= column * jnp.broadcast_to(panel[k : k + 1], (8, RANK))
                rows[m][p + 1] = total
            if p < 14:
                rest = jnp.concatenate(rows[m][p + 2 :], axis=0)
                pieces = [panel]
                if lo > 0:
                    pieces = [jnp.zeros((lo, RANK), F32)] + pieces
                pieces = pieces + [jnp.zeros((RANK - lo - 8, RANK), F32)]
                product = jnp.dot(
                    rest, jnp.concatenate(pieces, axis=0), precision=HIGHEST, preferred_element_type=F32
                )
                for i in range(p + 2, 16):
                    rows[m][i] = jnp.where(inside, 0.0, rows[m][i]) - product[8 * (i - p - 2) : 8 * (i - p - 1)]
    return [jnp.concatenate(d, axis=0) for d in done]


def factor_kernel(mine, projected, inverses, ortho):
    for m, inverse in enumerate(invert(unpack_symmetric(mine[HALF], mine[HALF + 1]))):
        inverses[m] = inverse
        ih, il = split(inverse)
        ph, plow = split(projected[m])
        ortho[m] = dot(ph, ih, (1, 1)) + dot(ph, il, (1, 1)) + dot(plow, ih, (1, 1))


def factor(mine, projected):
    return pl.pallas_call(
        factor_kernel,
        in_specs=[VMEM] * 2,
        out_specs=[VMEM] * 2,
        out_shape=[
            jax.ShapeDtypeStruct((3, RANK, RANK), F32),
            jax.ShapeDtypeStruct((3, 512, RANK), F32),
        ],
        compiler_params=pltpu.CompilerParams(vmem_limit_bytes=VMEM_LIMIT),
        cost_estimate=pl.CostEstimate(
            flops=6_000_000_000, bytes_accessed=3_000_000, transcendentals=0
        ),
        name="factor",
    )(mine, projected)


def rotate_kernel(mine, other, inverses, right_high, right_low, squares, sq, sk, sv, turned):
    fsdp = lax.axis_index("fsdp")
    core = lax.rem(fsdp, 2)

    def block(j):
        return jnp.where(core == j // HALF, mine[j % HALF], other[j % HALF])

    groups = ((0, range(0, 4)), (0, range(4, 8)), (0, range(8, 12)), (0, range(12, 16)))
    terms = [split(inverses[m]) for m in range(3)]
    stacked = [jnp.concatenate(pair, axis=0) for pair in terms]
    totals = [jnp.zeros((RANK, RANK), F32)] * 3
    for m, blocks in groups + ((1, (16,)), (2, (17,))):
        zh, zl = split(jnp.concatenate([block(j) for j in blocks], axis=1))
        both = dot(stacked[m], zh)
        right = both[:RANK] + both[RANK:] + dot(terms[m][0], zl)
        span = slice(RANK * blocks[0], RANK * blocks[-1] + RANK)
        right_high[:, span], right_low[:, span] = split(right)
        for i, j in enumerate(blocks):
            piece = right[:, RANK * i : RANK * i + RANK]
            totals[m] += piece * piece
            turned[j] = piece
    for m in range(3):
        sums = jnp.sum(totals[m].T, axis=0, keepdims=True)
        for d in range(8):
            squares[d, m : m + 1, :] = sums
    for d in range(8):
        squares[d, 3:, :] = jnp.zeros((5, RANK), F32)
    turned[0] = turned[lax.div(fsdp, 2)].T
    turned[1] = turned[16].T
    turned[2] = turned[17].T
    odd = lax.rem(fsdp, 2)
    sq[...] = turned[0, pl.ds(pl.multiple_of(odd * 64, 64), 64)]
    for m, out in ((1, sk), (2, sv)):
        tile = turned[m, pl.ds(pl.multiple_of(lax.div(fsdp, 2) * 8, 8), 8)]
        out[...] = jnp.where(odd == 0, tile[:4], tile[4:])


def rotate(mine, other, inverses):
    return pl.pallas_call(
        rotate_kernel,
        in_specs=[VMEM] * 3,
        out_specs=[VMEM] * 6,
        out_shape=[
            jax.ShapeDtypeStruct((RANK, 2304), BF16),
            jax.ShapeDtypeStruct((RANK, 2304), BF16),
            jax.ShapeDtypeStruct((8, 8, RANK), F32),
            jax.ShapeDtypeStruct((64, RANK), F32),
            jax.ShapeDtypeStruct((4, RANK), F32),
            jax.ShapeDtypeStruct((4, RANK), F32),
        ],
        scratch_shapes=[pltpu.VMEM((18, RANK, RANK), F32)],
        compiler_params=pltpu.CompilerParams(vmem_limit_bytes=VMEM_LIMIT),
        name="rotate",
    )(mine, other, inverses)


def update_kernel(
    factors, high, low, wq, wk, wv, ortho, rh, rl, squares, sq, sk, sv,
    mq, mk, mv, out_q, out_k, out_v, bq, bk, bv, lhs,
):
    step = pl.program_id(0)

    def new(m, span, weight, moment_out, weight_out):
        right = jnp.concatenate([rh[:, span], rh[:, span]], axis=0)
        low_right = rl[:, span]

        def product(at):
            return dot(lhs[m, at : at + 256], right) + dot(lhs[m, at : at + 256, :RANK], low_right)

        for at in (0, 256):
            part = slice(at, at + 256)
            blend = high[part, span].astype(F32) + low[part, span].astype(F32)
            moment_out[part] = (blend - product(at)).astype(BF16)
            weight_out[part] = (weight[part].astype(F32) - product(512 + at)).astype(BF16)

    @pl.when(step == 0)
    def _():
        inverse = lax.rsqrt(jnp.sum(squares[...], axis=0) + 1e-06)
        for m in range(3):
            scale = factors[m] * inverse[m : m + 1]
            for at, left in ((0, 0.5 * ortho[m]), (512, ortho[m] * scale)):
                h, l = split(left)
                lhs[m, at : at + 512, :RANK] = h
                lhs[m, at : at + 512, RANK:] = l
        for m, share, out in ((0, sq, bq), (1, sk, bk), (2, sv, bv)):
            out[...] = share[...] * inverse[m : m + 1]
        new(1, slice(2048, 2176), wk[...], mk, out_k)
        new(2, slice(2176, 2304), wv[...], mv, out_v)

    span = pl.ds(pl.multiple_of(step * WIDTH, WIDTH), WIDTH)
    new(0, span, wq[:, span], mq, out_q)


WIDTH = 2048 // STEPS
WIDE_SPECS = [column_spec(512), full_spec((512, RANK)), full_spec((512, RANK))]
WIDE_OUT = [
    jax.ShapeDtypeStruct((512, 2048), BF16),
    jax.ShapeDtypeStruct((512, RANK), BF16),
    jax.ShapeDtypeStruct((512, RANK), BF16),
]


def updates(factors, high, low, weights, ortho, rh, rl, squares, shares):
    share_specs = [full_spec((64, RANK)), full_spec((4, RANK)), full_spec((4, RANK))]
    return pl.pallas_call(
        functools.partial(update_kernel, factors),
        grid=(STEPS,),
        in_specs=[VMEM] * 12,
        out_specs=WIDE_SPECS + WIDE_SPECS + share_specs,
        out_shape=WIDE_OUT + WIDE_OUT + [jax.ShapeDtypeStruct(s.block_shape, F32) for s in share_specs],
        scratch_shapes=[pltpu.VMEM((3, 1024, 2 * RANK), BF16)],
        compiler_params=pltpu.CompilerParams(vmem_limit_bytes=VMEM_LIMIT),
        cost_estimate=pl.CostEstimate(
            flops=12 * 512 * 2304 * RANK, bytes_accessed=16_000_000, transcendentals=0
        ),
        name="updates",
    )(high, low, *weights, ortho, rh, rl, squares, *shares)


def body(
    weight_q,
    momentum_q,
    grad_q,
    basis_q,
    weight_k,
    momentum_k,
    grad_k,
    basis_k,
    weight_v,
    momentum_v,
    grad_v,
    basis_v,
):
    weights = (weight_q, weight_k, weight_v)
    moments = (momentum_q, momentum_k, momentum_v)
    grads = (grad_q, grad_k, grad_v)
    factors = [
        0.25 * math.sqrt(w.shape[0] * lax.axis_size("fsdp") * w.shape[1] * lax.axis_size("tensor") / RANK)
        for w in weights
    ]

    bases = jnp.concatenate([basis_q, basis_k, basis_v], axis=0)
    sibling, momentum_q = lax.optimization_barrier((swap_core(bases), momentum_q))
    early = early_blend_terms((momentum_q, momentum_k, momentum_v), grads)
    bases = small_kernel(repeat_kernel, (16, 144, RANK), "repeat_bases", bases, sibling)
    bases, early = lax.optimization_barrier((bases, early))
    gathered = plane_exchange(bases)
    high, low = blend_terms(moments, grads, early)
    gathered, high, low = lax.optimization_barrier((gathered, high, low))
    chunks = partial_rows(high, low, gathered)
    own = small_kernel(repeat_total_kernel, chunks.shape, "own_rows", tensor_exchange(chunks))
    rows = tensor_exchange(own)
    send, projected, lhs, grams = part_to_send(high, low, rows)
    sent = swap_core(send)
    keep = part_to_keep(high, low, lhs, grams)

    paired = small_kernel(pair_kernel, send.shape, "pair_sum", keep, sent)
    share = plane_exchange(paired.reshape(16, 88, RANK))
    share = small_kernel(repeat_total_kernel, (16, 88, RANK), "own_share", share)
    mine = plane_exchange(share).reshape(send.shape)
    other = swap_core(mine)
    inverses, ortho = factor(mine, projected)
    rh, rl, squares, *shares = rotate(mine, other, inverses)
    squares = tensor_exchange(squares)
    out = updates(factors, high, low, weights, ortho, rh, rl, squares, shares)
    return tuple(out[3 * j + i] for i in range(3) for j in (1, 0, 2))


def solution(mesh):
    placed = (
        P("fsdp", "tensor"),
        P("fsdp", "tensor"),
        P("fsdp", "tensor"),
        P(("tensor", "fsdp"), None),
    ) * 3
    return jax.shard_map(
        body,
        mesh=mesh,
        in_specs=placed,
        out_specs=(
            P("fsdp", "tensor"),
            P("fsdp", "tensor"),
            P(("tensor", "fsdp"), None),
        )
        * 3,
        check_vma=False,
    )
```

```python
import functools
import math

import jax
import jax.numpy as jnp
from jax import lax
from jax.experimental import pallas as pl
from jax.experimental.pallas import tpu as pltpu
from jax.sharding import PartitionSpec as P

RANK = 128
HIGHEST = lax.Precision.HIGHEST
F32 = jnp.float32
BF16 = jnp.bfloat16
PLANE = [[2 * i + c for i in range(16)] for c in range(2)]
SIBLING = [(i, i ^ 1) for i in range(32)]
STEPS = 2
HALF = 9
SUMMED = HALF + 2
VMEM_LIMIT = 24 * 1024 * 1024
EARLY_LIMIT = 60 * 1024 * 1024
BLEND_LIMIT = 46 * 1024 * 1024


def swap_core(x):
    return lax.ppermute(x, "fsdp", SIBLING)


def plane_exchange(x):
    return lax.all_to_all(x, "fsdp", 0, 0, tiled=True, axis_index_groups=PLANE)


def tensor_exchange(x):
    return lax.all_to_all(x, "tensor", 0, 0, tiled=True)


def dot(a, b, contract=(1, 0)):
    dims = (((contract[0],), (contract[1],)), ((), ()))
    return lax.dot_general(a, b, dims, preferred_element_type=F32)


def split(x):
    high = x.astype(BF16)
    return high, (x - high.astype(F32)).astype(BF16)


def blend_of(moment_ref, grad_ref):
    return moment_ref[...].astype(F32) + grad_ref[...].astype(F32)


def full_spec(shape):
    return pl.BlockSpec(shape, lambda i: (0,) * len(shape))


def column_spec(rows):
    return pl.BlockSpec((rows, 2048 // STEPS), lambda i: (0, i))


VMEM = pl.BlockSpec(memory_space=pltpu.VMEM)


SPLITS = ((0, 2048), (2048, 2176), (2176, 2304))
TERMS = [jax.ShapeDtypeStruct((512, 2304), BF16)] * 2


def early_blend_kernel(
    mq, gq, mk, gk, mv, gv, high_out, low_out, moments, grads, high, low, sems, out_sems
):
    @pl.when(lax.rem(lax.axis_index("fsdp"), 2) == 0)
    def _():
        halves = (slice(0, 256), slice(256, 512))
        fetches = [[], []]
        for h, rows in enumerate(halves):
            for i, ((lo, hi), moment, grad) in enumerate(zip(SPLITS, (mq, mk, mv), (gq, gk, gv))):
                for j, (source, target) in enumerate(((moment, moments), (grad, grads))):
                    copy = pltpu.make_async_copy(
                        source.at[rows], target.at[rows, lo:hi], sems.at[h, i, j]
                    )
                    copy.start()
                    fetches[h].append(copy)
        stores = []
        for h, rows in enumerate(halves):
            for copy in fetches[h]:
                copy.wait()
            for at in range(rows.start, rows.stop, 64):
                part = slice(at, at + 64)
                high[part], low[part] = split(moments[part].astype(F32) + grads[part].astype(F32))
            for j, (source, target) in enumerate(((high, high_out), (low, low_out))):
                copy = pltpu.make_async_copy(source.at[rows], target.at[rows], out_sems.at[h, j])
                copy.start()
                stores.append(copy)
        for copy in stores:
            copy.wait()


def early_blend_terms(moments, grads):
    anywhere = pl.BlockSpec(memory_space=pl.ANY)
    return pl.pallas_call(
        early_blend_kernel,
        in_specs=[anywhere] * 6,
        out_specs=[anywhere] * 2,
        out_shape=TERMS,
        scratch_shapes=[pltpu.VMEM((512, 2304), BF16)] * 4
        + [pltpu.SemaphoreType.DMA((2, 3, 2)), pltpu.SemaphoreType.DMA((2, 2))],
        compiler_params=pltpu.CompilerParams(vmem_limit_bytes=EARLY_LIMIT),
        name="early_blend_terms",
    )(*(x for group in zip(moments, grads) for x in group))


def blend_kernel(mq, gq, mk, gk, mv, gv, early_high, early_low, high, low, sems):
    core = lax.rem(lax.axis_index("fsdp"), 2)

    @pl.when(core == 0)
    def _():
        copies = [
            pltpu.make_async_copy(early_high, high, sems.at[0]),
            pltpu.make_async_copy(early_low, low, sems.at[1]),
        ]
        for copy in copies:
            copy.start()
        for copy in copies:
            copy.wait()

    @pl.when(core == 1)
    def _():
        for (lo, hi), moment, grad in zip(SPLITS, (mq, mk, mv), (gq, gk, gv)):
            for at in range(0, 512, 64):
                part = slice(at, at + 64)
                blend = moment[part].astype(F32) + grad[part].astype(F32)
                high[part, lo:hi], low[part, lo:hi] = split(blend)


def blend_terms(moments, grads, early):
    return pl.pallas_call(
        blend_kernel,
        in_specs=[VMEM] * 6 + [pl.BlockSpec(memory_space=pl.ANY)] * 2,
        out_specs=[VMEM] * 2,
        out_shape=TERMS,
        scratch_shapes=[pltpu.SemaphoreType.DMA((2,))],
        compiler_params=pltpu.CompilerParams(vmem_limit_bytes=BLEND_LIMIT),
        cost_estimate=pl.CostEstimate(
            flops=4 * 512 * 2304, bytes_accessed=14_000_000, transcendentals=0
        ),
        name="blend_terms",
    )(*(x for group in zip(moments, grads) for x in group), *early)


def small_kernel(kernel, shape, name, *operands):
    return pl.pallas_call(
        kernel,
        in_specs=[VMEM] * len(operands),
        out_specs=VMEM,
        out_shape=jax.ShapeDtypeStruct(shape, F32),
        compiler_params=pltpu.CompilerParams(vmem_limit_bytes=VMEM_LIMIT),
        name=name,
    )(*operands)


def repeat_kernel(own, sibling, out):
    first = lax.rem(lax.axis_index("fsdp"), 2) == 0
    a, b = own[...], sibling[...]
    low, high = jnp.where(first, a, b), jnp.where(first, b, a)
    for i in range(out.shape[0]):
        out[i, :72] = low
        out[i, 72:] = high


def repeat_total_kernel(parts, out):
    total = jnp.sum(parts[...], axis=0)
    for i in range(out.shape[0]):
        out[i] = total


def pair_kernel(a, b, out):
    out[...] = a[...] + b[...]


def high_rows_kernel(high, gathered, out, basis, small):
    for i in range(16):
        pair = (gathered[i, :72], gathered[i, 72:])
        for c in range(2):
            at = 128 * i + 64 * c
            qh, ql = split(pair[c][:64])
            basis[at : at + 64, :RANK] = qh
            basis[at : at + 64, RANK:] = ql
        for n in range(2):
            piece = [x[64 + 4 * n : 68 + 4 * n] for x in pair]
            small[n, 8 * i : 8 * i + 8] = jnp.concatenate(piece, axis=0)
    for n in range(2):
        qh, ql = split(small[n])
        basis[2048 + RANK * n : 2048 + RANK * n + RANK, :RANK] = qh
        basis[2048 + RANK * n : 2048 + RANK * n + RANK, RANK:] = ql
    for m, (lo, hi) in enumerate(SPLITS):
        for half in range(2):
            both = dot(high[256 * half : 256 * half + 256, lo:hi], basis[lo:hi])
            rows = both[:, :RANK] + both[:, RANK:]
            for d in range(4):
                out[4 * half + d, 64 * m : 64 * m + 64] = rows[64 * d : 64 * d + 64]


def low_rows_kernel(low, basis, part, out):
    for m, (lo, hi) in enumerate(SPLITS):
        for half in range(2):
            rows = dot(low[256 * half : 256 * half + 256, lo:hi], basis[lo:hi, :RANK])
            for d in range(4):
                at = (4 * half + d, slice(64 * m, 64 * m + 64))
                out[at] = part[at] + rows[64 * d : 64 * d + 64]


ROWS_SHAPE = jax.ShapeDtypeStruct((8, 192, RANK), F32)


def partial_rows(high, low, gathered):
    params = pltpu.CompilerParams(vmem_limit_bytes=VMEM_LIMIT)
    part, basis = pl.pallas_call(
        high_rows_kernel,
        in_specs=[VMEM] * 2,
        out_specs=[VMEM] * 2,
        out_shape=[ROWS_SHAPE, jax.ShapeDtypeStruct((2304, 2 * RANK), BF16)],
        scratch_shapes=[pltpu.VMEM((2, RANK, RANK), F32)],
        compiler_params=params,
        cost_estimate=pl.CostEstimate(
            flops=4 * 512 * 2304 * RANK, bytes_accessed=7_000_000, transcendentals=0
        ),
        name="high_rows",
    )(high, gathered)
    return pl.pallas_call(
        low_rows_kernel,
        in_specs=[VMEM] * 3,
        out_specs=VMEM,
        out_shape=ROWS_SHAPE,
        compiler_params=params,
        cost_estimate=pl.CostEstimate(
            flops=2 * 512 * 2304 * RANK, bytes_accessed=4_000_000, transcendentals=0
        ),
        name="low_rows",
    )(low, basis, part)


def grid_of_indices():
    row = lax.broadcasted_iota(jnp.int32, (RANK, RANK), 0)
    return row, lax.broadcasted_iota(jnp.int32, (RANK, RANK), 1)


def pack_symmetric(a, b, c):
    row, col = grid_of_indices()
    diagonal = jnp.sum(jnp.where(row == col, b, 0.0), axis=0, keepdims=True)
    first = jnp.where(row >= col, a, b.T)
    upper = jnp.where((row == 0) & (col > 0), diagonal, 0.0)
    upper = jnp.where((row == 1) & (col == RANK - 1), b[:1, :1], upper)
    return first, jnp.where(row >= col, c, upper)


def unpack_symmetric(first, second):
    row, col = grid_of_indices()
    turned = first.T
    diagonal = jnp.where(col[:1] == 0, second[1:2, RANK - 1 :], second[:1])
    a = jnp.where(row >= col, first, turned)
    b = jnp.where(row < col, first, jnp.where(row > col, turned, diagonal))
    return a, b, jnp.where(row >= col, second, second.T)


def half_of_right(half, high, low, lhs, out):
    def times(m, lo, hi):
        both = dot(lhs[m], high[:, lo:hi])
        return both[:RANK] + both[RANK:] + dot(lhs[m, :RANK], low[:, lo:hi])

    first = HALF * half
    for lo in range(first, min(first + HALF, 16), 3):
        hi = min(lo + 3, first + HALF, 16)
        right = times(0, RANK * lo, RANK * hi)
        for i in range(hi - lo):
            out[lo - first + i] = right[:, RANK * i : RANK * i + RANK]
    if half == 1:
        out[16 - HALF] = times(1, 2048, 2176)
        out[17 - HALF] = times(2, 2176, 2304)


def send_kernel(high, low, rows, send, projected, lhs, grams):
    for d in range(8):
        for m in range(3):
            projected[m, 64 * d : 64 * d + 64] = rows[d, 64 * m : 64 * m + 64]
    squares = []
    for m in range(3):
        p = projected[m]
        turned = p.T
        h, l = split(turned)
        lhs[m, :RANK] = h
        lhs[m, RANK:] = l
        squares.append(jnp.dot(turned, p, precision=HIGHEST, preferred_element_type=F32))
    core = lax.rem(lax.axis_index("fsdp"), 2)
    for half in range(2):
        pl.when(core != half)(functools.partial(half_of_right, half, high, low, lhs, send))
    for i, block in enumerate(pack_symmetric(*squares)):
        send[HALF + i] = block
        grams[i] = block


def keep_kernel(high, low, lhs, grams, keep):
    core = lax.rem(lax.axis_index("fsdp"), 2)
    for half in range(2):
        pl.when(core == half)(functools.partial(half_of_right, half, high, low, lhs, keep))
    for i in range(2):
        keep[HALF + i] = grams[i]


HALF_SHAPE = jax.ShapeDtypeStruct((SUMMED, RANK, RANK), F32)
HALF_COST = pl.CostEstimate(
    flops=3 * 512 * 2304 * RANK, bytes_accessed=5_000_000, transcendentals=0
)


def part_to_send(high, low, rows):
    return pl.pallas_call(
        send_kernel,
        in_specs=[VMEM] * 3,
        out_specs=[VMEM] * 4,
        out_shape=[
            HALF_SHAPE,
            jax.ShapeDtypeStruct((3, 512, RANK), F32),
            jax.ShapeDtypeStruct((3, 2 * RANK, 512), BF16),
            jax.ShapeDtypeStruct((2, RANK, RANK), F32),
        ],
        compiler_params=pltpu.CompilerParams(vmem_limit_bytes=VMEM_LIMIT),
        cost_estimate=HALF_COST,
        name="part_to_send",
    )(high, low, rows)


def part_to_keep(high, low, lhs, grams):
    return pl.pallas_call(
        keep_kernel,
        in_specs=[VMEM] * 4,
        out_specs=VMEM,
        out_shape=HALF_SHAPE,
        compiler_params=pltpu.CompilerParams(vmem_limit_bytes=VMEM_LIMIT),
        cost_estimate=HALF_COST,
        name="part_to_keep",
    )(high, low, lhs, grams)


def invert(grams):
    sub = lax.broadcasted_iota(jnp.int32, (8, RANK), 0)
    lane = lax.broadcasted_iota(jnp.int32, (8, RANK), 1)
    count = len(grams)
    rows = [[g[8 * p : 8 * p + 8] for p in range(16)] for g in grams]
    done = [[] for _ in grams]
    for p in range(16):
        lo = 8 * p
        for m in range(count):
            panel = rows[m][p]
            cols = [jnp.broadcast_to(panel[:, lo + k : lo + k + 1], (8, RANK)) for k in range(8)]
            inverse = jnp.zeros((8, RANK), F32)
            for j in range(8):
                at = sub == j
                here = lane == lo + j
                root = lax.rsqrt(jnp.broadcast_to(cols[j][j : j + 1], (8, RANK)))
                scale = root * root
                row = jnp.where(here, 1.0, jnp.broadcast_to(panel[j : j + 1], (8, RANK)))
                inverse = jnp.where(at, row * root, inverse)
                row = row * scale
                panel = jnp.where(at, row, jnp.where(here, 0.0, panel) - cols[j] * row)
                for k in range(j + 1, 8):
                    entry = jnp.broadcast_to(cols[k][j : j + 1], (8, RANK)) * scale
                    cols[k] = jnp.where(at, entry, cols[k] - cols[j] * entry)
            done[m].append(jnp.where(lane <= sub + lo, inverse, 0.0))
            inside = (lane >= lo) & (lane < lo + 8)
            if p < 15:
                ahead = rows[m][p + 1]
                total = jnp.where(inside, 0.0, ahead)
                for k in range(8):
                    column = jnp.broadcast_to(ahead[:, lo + k : lo + k + 1], (8, RANK))
                    total -= column * jnp.broadcast_to(panel[k : k + 1], (8, RANK))
                rows[m][p + 1] = total
            if p < 14:
                rest = jnp.concatenate(rows[m][p + 2 :], axis=0)
                pieces = [panel]
                if lo > 0:
                    pieces = [jnp.zeros((lo, RANK), F32)] + pieces
                pieces = pieces + [jnp.zeros((RANK - lo - 8, RANK), F32)]
                product = jnp.dot(
                    rest, jnp.concatenate(pieces, axis=0), precision=HIGHEST, preferred_element_type=F32
                )
                for i in range(p + 2, 16):
                    rows[m][i] = jnp.where(inside, 0.0, rows[m][i]) - product[8 * (i - p - 2) : 8 * (i - p - 1)]
    return [jnp.concatenate(d, axis=0) for d in done]


def factor_kernel(mine, projected, inverses, ortho):
    for m, inverse in enumerate(invert(unpack_symmetric(mine[HALF], mine[HALF + 1]))):
        inverses[m] = inverse
        ih, il = split(inverse)
        ph, plow = split(projected[m])
        ortho[m] = dot(ph, ih, (1, 1)) + dot(ph, il, (1, 1)) + dot(plow, ih, (1, 1))


def factor(mine, projected):
    return pl.pallas_call(
        factor_kernel,
        in_specs=[VMEM] * 2,
        out_specs=[VMEM] * 2,
        out_shape=[
            jax.ShapeDtypeStruct((3, RANK, RANK), F32),
            jax.ShapeDtypeStruct((3, 512, RANK), F32),
        ],
        compiler_params=pltpu.CompilerParams(vmem_limit_bytes=VMEM_LIMIT),
        cost_estimate=pl.CostEstimate(
            flops=6_000_000_000, bytes_accessed=3_000_000, transcendentals=0
        ),
        name="factor",
    )(mine, projected)


def rotate_kernel(mine, other, inverses, right_high, right_low, squares, sq, sk, sv, turned):
    fsdp = lax.axis_index("fsdp")
    core = lax.rem(fsdp, 2)

    def block(j):
        return jnp.where(core == j // HALF, mine[j % HALF], other[j % HALF])

    groups = ((0, range(0, 4)), (0, range(4, 8)), (0, range(8, 12)), (0, range(12, 16)))
    terms = [split(inverses[m]) for m in range(3)]
    stacked = [jnp.concatenate(pair, axis=0) for pair in terms]
    totals = [jnp.zeros((RANK, RANK), F32)] * 3
    for m, blocks in groups + ((1, (16,)), (2, (17,))):
        zh, zl = split(jnp.concatenate([block(j) for j in blocks], axis=1))
        both = dot(stacked[m], zh)
        right = both[:RANK] + both[RANK:] + dot(terms[m][0], zl)
        span = slice(RANK * blocks[0], RANK * blocks[-1] + RANK)
        right_high[:, span], right_low[:, span] = split(right)
        for i, j in enumerate(blocks):
            piece = right[:, RANK * i : RANK * i + RANK]
            totals[m] += piece * piece
            turned[j] = piece
    for m in range(3):
        sums = jnp.sum(totals[m].T, axis=0, keepdims=True)
        for d in range(8):
            squares[d, m : m + 1, :] = sums
    for d in range(8):
        squares[d, 3:, :] = jnp.zeros((5, RANK), F32)
    turned[0] = turned[lax.div(fsdp, 2)].T
    turned[1] = turned[16].T
    turned[2] = turned[17].T
    odd = lax.rem(fsdp, 2)
    sq[...] = turned[0, pl.ds(pl.multiple_of(odd * 64, 64), 64)]
    for m, out in ((1, sk), (2, sv)):
        tile = turned[m, pl.ds(pl.multiple_of(lax.div(fsdp, 2) * 8, 8), 8)]
        out[...] = jnp.where(odd == 0, tile[:4], tile[4:])


def rotate(mine, other, inverses):
    return pl.pallas_call(
        rotate_kernel,
        in_specs=[VMEM] * 3,
        out_specs=[VMEM] * 6,
        out_shape=[
            jax.ShapeDtypeStruct((RANK, 2304), BF16),
            jax.ShapeDtypeStruct((RANK, 2304), BF16),
            jax.ShapeDtypeStruct((8, 8, RANK), F32),
            jax.ShapeDtypeStruct((64, RANK), F32),
            jax.ShapeDtypeStruct((4, RANK), F32),
            jax.ShapeDtypeStruct((4, RANK), F32),
        ],
        scratch_shapes=[pltpu.VMEM((18, RANK, RANK), F32)],
        compiler_params=pltpu.CompilerParams(vmem_limit_bytes=VMEM_LIMIT),
        name="rotate",
    )(mine, other, inverses)


def update_kernel(
    factors, high, low, wq, wk, wv, ortho, rh, rl, squares, sq, sk, sv,
    mq, mk, mv, out_q, out_k, out_v, bq, bk, bv, lhs,
):
    step = pl.program_id(0)

    def new(m, span, weight, moment_out, weight_out):
        right = jnp.concatenate([rh[:, span], rh[:, span]], axis=0)
        low_right = rl[:, span]

        def product(at):
            return dot(lhs[m, at : at + 256], right) + dot(lhs[m, at : at + 256, :RANK], low_right)

        for at in (0, 256):
            part = slice(at, at + 256)
            blend = high[part, span].astype(F32) + low[part, span].astype(F32)
            moment_out[part] = (blend - product(at)).astype(BF16)
            weight_out[part] = (weight[part].astype(F32) - product(512 + at)).astype(BF16)

    @pl.when(step == 0)
    def _():
        inverse = lax.rsqrt(jnp.sum(squares[...], axis=0) + 1e-06)
        for m in range(3):
            scale = factors[m] * inverse[m : m + 1]
            for at, left in ((0, 0.5 * ortho[m]), (512, ortho[m] * scale)):
                h, l = split(left)
                lhs[m, at : at + 512, :RANK] = h
                lhs[m, at : at + 512, RANK:] = l
        for m, share, out in ((0, sq, bq), (1, sk, bk), (2, sv, bv)):
            out[...] = share[...] * inverse[m : m + 1]
        new(1, slice(2048, 2176), wk[...], mk, out_k)
        new(2, slice(2176, 2304), wv[...], mv, out_v)

    span = pl.ds(pl.multiple_of(step * WIDTH, WIDTH), WIDTH)
    new(0, span, wq[:, span], mq, out_q)


WIDTH = 2048 // STEPS
WIDE_SPECS = [column_spec(512), full_spec((512, RANK)), full_spec((512, RANK))]
WIDE_OUT = [
    jax.ShapeDtypeStruct((512, 2048), BF16),
    jax.ShapeDtypeStruct((512, RANK), BF16),
    jax.ShapeDtypeStruct((512, RANK), BF16),
]


def updates(factors, high, low, weights, ortho, rh, rl, squares, shares):
    share_specs = [full_spec((64, RANK)), full_spec((4, RANK)), full_spec((4, RANK))]
    return pl.pallas_call(
        functools.partial(update_kernel, factors),
        grid=(STEPS,),
        in_specs=[VMEM] * 12,
        out_specs=WIDE_SPECS + WIDE_SPECS + share_specs,
        out_shape=WIDE_OUT + WIDE_OUT + [jax.ShapeDtypeStruct(s.block_shape, F32) for s in share_specs],
        scratch_shapes=[pltpu.VMEM((3, 1024, 2 * RANK), BF16)],
        compiler_params=pltpu.CompilerParams(vmem_limit_bytes=VMEM_LIMIT),
        cost_estimate=pl.CostEstimate(
            flops=12 * 512 * 2304 * RANK, bytes_accessed=16_000_000, transcendentals=0
        ),
        name="updates",
    )(high, low, *weights, ortho, rh, rl, squares, *shares)


def body(
    weight_q,
    momentum_q,
    grad_q,
    basis_q,
    weight_k,
    momentum_k,
    grad_k,
    basis_k,
    weight_v,
    momentum_v,
    grad_v,
    basis_v,
):
    weights = (weight_q, weight_k, weight_v)
    moments = (momentum_q, momentum_k, momentum_v)
    grads = (grad_q, grad_k, grad_v)
    factors = [
        0.25 * math.sqrt(w.shape[0] * lax.axis_size("fsdp") * w.shape[1] * lax.axis_size("tensor") / RANK)
        for w in weights
    ]

    bases = jnp.concatenate([basis_q, basis_k, basis_v], axis=0)
    sibling, momentum_q = lax.optimization_barrier((swap_core(bases), momentum_q))
    early = early_blend_terms((momentum_q, momentum_k, momentum_v), grads)
    bases = small_kernel(repeat_kernel, (16, 144, RANK), "repeat_bases", bases, sibling)
    bases, early = lax.optimization_barrier((bases, early))
    gathered = plane_exchange(bases)
    high, low = blend_terms(moments, grads, early)
    gathered, high, low = lax.optimization_barrier((gathered, high, low))
    chunks = partial_rows(high, low, gathered)
    own = small_kernel(repeat_total_kernel, chunks.shape, "own_rows", tensor_exchange(chunks))
    rows = tensor_exchange(own)
    send, projected, lhs, grams = part_to_send(high, low, rows)
    sent = swap_core(send)
    keep = part_to_keep(high, low, lhs, grams)

    paired = small_kernel(pair_kernel, send.shape, "pair_sum", keep, sent)
    share = plane_exchange(paired.reshape(16, 88, RANK))
    share = small_kernel(repeat_total_kernel, (16, 88, RANK), "own_share", share)
    mine = plane_exchange(share).reshape(send.shape)
    other = swap_core(mine)
    inverses, ortho = factor(mine, projected)
    rh, rl, squares, *shares = rotate(mine, other, inverses)
    squares = tensor_exchange(squares)
    out = updates(factors, high, low, weights, ortho, rh, rl, squares, shares)
    return tuple(out[3 * j + i] for i in range(3) for j in (1, 0, 2))


def solution(mesh):
    placed = (
        P("fsdp", "tensor"),
        P("fsdp", "tensor"),
        P("fsdp", "tensor"),
        P(("tensor", "fsdp"), None),
    ) * 3
    return jax.shard_map(
        body,
        mesh=mesh,
        in_specs=placed,
        out_specs=(
            P("fsdp", "tensor"),
            P("fsdp", "tensor"),
            P(("tensor", "fsdp"), None),
        )
        * 3,
        check_vma=False,
    )
```
